128 devices in a mesh: row: 16 (over x, z), col: 8 (over y, core).
Axes of the slice: x: 4, y: 4, z: 4, core: 2. Of those that a mesh axis runs over, the one named last changes fastest.
Arguments:
- tokens: bfloat16 [1024, 8192], P('col', 'row'), may hold values from -6 to 6
- gate_weight: bfloat16 [8192, 14336], P('row', 'col'), may hold values from -0.09375 to 0.09375
- up_weight: bfloat16 [8192, 14336], P('row', 'col'), may hold values from -0.09375 to 0.09375
- down_weight: bfloat16 [14336, 8192], P('col', 'row'), may hold values from -0.09375 to 0.09375
- gate_mask: int32 [128, 224], P('row', 'col'), may hold values from 0 to 1, as said below
- up_mask: int32 [128, 224], P('row', 'col'), may hold values from 0 to 1, as said below
- down_mask: int32 [224, 128], P('col', 'row'), may hold values from 0 to 1, as said below
- head_weight: bfloat16 [8192, 128], P('row'), may hold values from -0.15625 to 0.15625
- labels: int32 [1024], P('col'), may hold values from 0 to 127
Outputs:
- token_loss: float32 [1024], P('col')
- tokens_grad: bfloat16 [1024, 8192], P('col', 'row')
- gate_grad: bfloat16 [8192, 14336], P('row', 'col')
- up_grad: bfloat16 [8192, 14336], P('row', 'col')
- down_grad: bfloat16 [14336, 8192], P('col', 'row')
The draws below stay inside these ranges and needn't reach their ends.
Inputs may be any that keep to these rules, and one draw needn't show every extreme that they name: `gate_mask`: 1 keeps a block of 64 x 64 weights, 0 prunes it. `up_mask`: 1 keeps a block of 64 x 64 weights, 0 prunes it. `down_mask`: 1 keeps a block of 64 x 64 weights, 0 prunes it.
All inputs are finite; a program needn't handle non-finite values.
Results may differ from the reference program's by a relative error of at most 0.011.
Values may be sent and summed in bfloat16 or wider, within the bound.
No kernel may reach another device: no remote copies, remote signals or barrier semaphores. Data moves between devices by JAX's collectives and lax.ppermute only.
A program may use at most 128 MiB of HBM per device.

```python
import jax
import jax.numpy as jnp
from jax import lax

D = 8192
FF = 14336
BLOCK = 64
CLASSES = 128
TOKENS = 1024


def keep_blocks(key, height, breadth, by_rows):
    level_key, pick_key = jax.random.split(key)
    if by_rows:
        level = jax.random.randint(level_key, (height, 1), 1, 4)
    else:
        level = jax.random.randint(level_key, (1, breadth), 1, 4)
    picks = jax.random.randint(pick_key, (height, breadth), 0, 4)
    return (picks < level).astype(jnp.int32)


def draw_gate_mask(key, part):
    return keep_blocks(jax.random.fold_in(key, 11), D // BLOCK, FF // BLOCK, True)


def draw_up_mask(key, part):
    return keep_blocks(jax.random.fold_in(key, 23), D // BLOCK, FF // BLOCK, True)


def draw_down_mask(key, part):
    return keep_blocks(jax.random.fold_in(key, 37), FF // BLOCK, D // BLOCK, False)


def touch_ends(array, key, least, high):
    longest = array.shape.index(max(array.shape))
    spots = []
    for shift in (0, 1):
        where = [jax.random.randint(jax.random.fold_in(key, axis), (), 0, length) for axis, length in enumerate(array.shape)]
        where[longest] = (where[longest] + shift) % array.shape[longest]
        spots.append(tuple(where))
    return array.at[spots[0]].set(least).at[spots[1]].set(high)


def levels(own_key, shape, shards, low, largest):
    gain = 1.0
    for axis_at, parts in shards:
        steps = jax.random.uniform(jax.random.fold_in(jax.random.fold_in(own_key, 6), axis_at), (parts,), jnp.float32, low / len(shards), largest / len(shards))
        gain = gain * jnp.repeat(jnp.exp(steps), shape[axis_at] // parts).reshape((-1,) + (1,) * (len(shape) - 1 - axis_at))
    return gain


def noise(stream_key, dims, spread, reach, shards=(), held_as=jnp.bfloat16):
    gain = levels(stream_key, dims, shards, -0.22, 0.18) if shards else 1.0
    entries = jax.random.normal(stream_key, dims, jnp.float32) * spread * gain
    return jnp.minimum(jnp.maximum(entries, -reach), reach).astype(held_as)


def setup_inputs(seed: int = 0) -> dict:
    arg_keys = jax.random.split(jax.random.key(seed), 10)
    return {
        "tokens": noise(arg_keys[0], (TOKENS, D), 1.0, 6.0, ((0, 8), (1, 16))),
        "gate_weight": noise(arg_keys[1], (D, FF), (D // 2) ** -0.5, 0.09375, ((0, 16), (1, 8))),
        "up_weight": noise(arg_keys[2], (D, FF), (D // 2) ** -0.5, 0.09375, ((0, 16), (1, 8))),
        "down_weight": noise(arg_keys[3], (FF, D), (FF // 4) ** -0.5, 0.09375, ((0, 8), (1, 16))),
        "gate_mask": draw_gate_mask(jax.random.fold_in(arg_keys[9], 71), 0),
        "up_mask": draw_up_mask(jax.random.fold_in(arg_keys[9], 71), 0),
        "down_mask": draw_down_mask(jax.random.fold_in(arg_keys[9], 71), 0),
        "head_weight": noise(arg_keys[7], (D, CLASSES), (D // 6) ** -0.5, 0.15625, ((0, 16),)),
        "labels": touch_ends(jax.random.randint(arg_keys[8], (TOKENS,), 0, CLASSES), jax.random.fold_in(arg_keys[8], 1), 0, CLASSES - 1).astype(jnp.int32),
    }


loss_scale = 8.0


def masked(weight, block_mask):
    height, breadth = weight.shape
    blocks = weight.reshape(block_mask.shape[0], height // block_mask.shape[0], block_mask.shape[1], breadth // block_mask.shape[1])
    pruned = blocks * block_mask[:, None, :, None].astype(weight.dtype)
    return pruned.reshape(height, breadth)


def classify(logits, labels):
    exponent = jnp.exp(logits)
    partition = jnp.sum(exponent, axis=1, keepdims=True)
    classes = lax.broadcasted_iota(jnp.int32, logits.shape, 1)
    onehot = (labels[:, None] == classes).astype(jnp.float32)
    token_cost = jnp.log(partition[:, 0]) - jnp.sum(logits * onehot, axis=1)
    return token_cost, loss_scale * (exponent / partition - onehot)


def reference(tokens, gate_weight, up_weight, down_weight, gate_mask, up_mask, down_mask, head_weight, labels):
    gate_kept = masked(gate_weight, gate_mask)
    up_kept = masked(up_weight, up_mask)
    down_kept = masked(down_weight, down_mask)
    gate_sum = jnp.dot(tokens, gate_kept, preferred_element_type=jnp.float32)
    up_sum = jnp.dot(tokens, up_kept, preferred_element_type=jnp.float32)
    sigmoid_gate = jax.nn.sigmoid(gate_sum)
    activated = gate_sum * sigmoid_gate
    hidden = (activated * up_sum).astype(jnp.bfloat16)
    mixed_rows = (tokens.astype(jnp.float32) + jnp.dot(hidden, down_kept, preferred_element_type=jnp.float32)).astype(jnp.bfloat16)
    logits = jnp.dot(mixed_rows, head_weight, preferred_element_type=jnp.float32)
    token_loss, grad_full = classify(logits, labels)
    dlogits = grad_full.astype(jnp.bfloat16)
    dmixed = jnp.dot(dlogits, head_weight.T, preferred_element_type=jnp.float32).astype(jnp.bfloat16)
    dhidden = jnp.dot(dmixed, down_kept.T, preferred_element_type=jnp.float32)
    gate_delta = (dhidden * up_sum * sigmoid_gate * (1.0 + gate_sum * (1.0 - sigmoid_gate))).astype(jnp.bfloat16)
    up_delta = (dhidden * activated).astype(jnp.bfloat16)
    down_grad = masked(jnp.dot(hidden.T, dmixed, preferred_element_type=jnp.float32), down_mask).astype(jnp.bfloat16)
    gate_grad = masked(jnp.dot(tokens.T, gate_delta, preferred_element_type=jnp.float32), gate_mask).astype(jnp.bfloat16)
    up_grad = masked(jnp.dot(tokens.T, up_delta, preferred_element_type=jnp.float32), up_mask).astype(jnp.bfloat16)
    input_sum = jnp.dot(gate_delta, gate_kept.T, preferred_element_type=jnp.float32) + jnp.dot(up_delta, up_kept.T, preferred_element_type=jnp.float32)
    tokens_grad = (dmixed.astype(jnp.float32) + input_sum).astype(jnp.bfloat16)
    return (token_loss, tokens_grad, gate_grad, up_grad, down_grad)
```

```python
import jax
import jax.numpy as jnp
from jax import lax
from jax.sharding import PartitionSpec as P

loss_scale = 8.0
bf16 = jnp.bfloat16
f32 = jnp.float32
block = 64


def kept_blocks(weight, block_mask):
    height, breadth = weight.shape
    lanes = jnp.repeat(block_mask.astype(weight.dtype), breadth // block_mask.shape[1], axis=1)
    tall = weight.reshape(block_mask.shape[0], height // block_mask.shape[0], breadth)
    return (tall * lanes[:, None, :]).reshape(height, breadth)


def shift(value, line, step):
    if line == "x":
        pairs = [(r, (r // 4 + step) % 4 * 4 + r % 4) for r in range(16)]
        return lax.ppermute(value, "row", pairs)
    if line == "z":
        pairs = [(r, r // 4 * 4 + (r % 4 + step) % 4) for r in range(16)]
        return lax.ppermute(value, "row", pairs)
    if line == "y":
        pairs = [(c, (c // 2 + step) % 4 * 2 + c % 2) for c in range(8)]
        return lax.ppermute(value, "col", pairs)
    return lax.ppermute(value, "col", [(c, c ^ 1) for c in range(8)])


def pick(stack, at, axis=0):
    return lax.dynamic_index_in_dim(stack, at % stack.shape[axis], axis, keepdims=False)


def put(stack, value, at):
    return lax.dynamic_update_index_in_dim(stack, value, at % stack.shape[0], 0)


def product(left, right):
    return jnp.dot(left, right, preferred_element_type=f32)


def product_t(left, right):
    return lax.dot_general(left, right, (((1,), (1,)), ((), ())), preferred_element_type=f32)


def t_product(left, right):
    return lax.dot_general(left, right, (((0,), (0,)), ((), ())), preferred_element_type=f32)


def ring_sum(rows_of, weight, line, at, other, other_at):
    half = rows_of(at).shape[0] // 2
    far = product(rows_of(at + 2), weight).astype(bf16)
    far_up = shift(far[:half], line, 1)
    far_down = shift(far[half:], line, -1)
    up_rows, down_rows = rows_of(at + 1), rows_of(at - 1)
    up_late = shift(product(up_rows[half:], weight).astype(bf16), line, 1)
    down_late = shift(product(down_rows[:half], weight).astype(bf16), line, -1)
    up_first = shift((product(up_rows[:half], weight) + far_up.astype(f32)).astype(bf16), line, 1)
    down_first = shift((product(down_rows[half:], weight) + far_down.astype(f32)).astype(bf16), line, -1)
    from_below = jnp.concatenate([up_first, up_late], axis=0).astype(f32)
    from_above = jnp.concatenate([down_late, down_first], axis=0).astype(f32)
    mine = product(rows_of(at), weight) + from_below + from_above
    parts = mine.reshape(4, mine.shape[0] // 4, mine.shape[1])
    got = [
        shift(pick(parts, other_at + step).astype(bf16), other, step) for step in (1, -1, 2)
    ]
    total = pick(parts, other_at)
    for value in got:
        total = total + value.astype(f32)
    return total


def ring_gather(mine, line, at, other, other_at):
    chunk = jnp.zeros((4,) + mine.shape, mine.dtype)
    chunk = put(chunk, mine, other_at)
    for step in (1, -1, 2):
        chunk = put(chunk, shift(mine, other, step), other_at - step)
    top, bottom = chunk[:2], chunk[2:]
    below_top = shift(top, line, 1)
    above_bottom = shift(bottom, line, -1)
    below_bottom = shift(bottom, line, 1)
    above_top = shift(top, line, -1)
    far_top = shift(below_top, line, 1)
    far_bottom = shift(above_bottom, line, -1)
    whole = jnp.zeros((4, 2, 2) + mine.shape, mine.dtype)
    whole = put(whole, chunk.reshape(2, 2, *mine.shape), at)
    whole = put(whole, jnp.stack([below_top, below_bottom]), at - 1)
    whole = put(whole, jnp.stack([above_top, above_bottom]), at + 1)
    whole = put(whole, jnp.stack([far_top, far_bottom]), at + 2)
    return whole.reshape(4, 4, *mine.shape)


def shards(
    tokens, gate_weight, up_weight, down_weight, gate_mask, up_mask, down_mask, head_weight, labels
):
    row, col = lax.axis_index("row"), lax.axis_index("col")
    x, z, y, core = row // 4, row % 4, col // 2, col % 2
    width = tokens.shape[1]
    own = tokens.shape[0]
    units = gate_weight.shape[1]
    half = units // 2
    count = own * 8
    rows = count // 16

    mates = put(jnp.zeros((4, own, width), bf16), tokens, y)
    for step in (1, -1, 2):
        mates = put(mates, shift(tokens, "y", step), y - step)
    others = shift(mates, "core", 1)
    first = core == 0
    every = jnp.stack([jnp.where(first, mates, others), jnp.where(first, others, mates)], axis=1)
    every = every.reshape(count, width)

    down_kept = kept_blocks(down_weight, down_mask)
    small = jnp.concatenate([product(down_kept, head_weight), product(tokens, head_weight)], axis=0)
    small = lax.psum(small, "row")
    down_head = small[:units].astype(bf16)
    token_head = small[units:]

    gate_kept = kept_blocks(gate_weight, gate_mask)
    up_kept = kept_blocks(up_weight, up_mask)
    weight_p = jnp.concatenate([gate_kept[:, :half], up_kept[:, :half]], axis=1)
    weight_q = jnp.concatenate([gate_kept[:, half:], up_kept[:, half:]], axis=1)
    grid = every.reshape(4, 4, rows, width)
    sum_p = ring_sum(lambda j: pick(grid, j, 0).reshape(4 * rows, width), weight_p, "x", x, "z", z)
    sum_q = ring_sum(lambda j: pick(grid, j, 1).reshape(4 * rows, width), weight_q, "z", z, "x", x)

    part = jnp.zeros((rows, head_weight.shape[1]), f32)
    for sums, side in ((sum_p, down_head[:half]), (sum_q, down_head[half:])):
        gate, up = sums[:, :half], sums[:, half:]
        part += product((gate * jax.nn.sigmoid(gate) * up).astype(bf16), side)
    owner = col == row // 2
    start = row % 2 * rows
    part += jnp.where(owner, lax.dynamic_slice_in_dim(token_head, start, rows, 0), 0.0)
    label_row = jnp.where(owner, lax.dynamic_slice_in_dim(labels, start, rows, 0), 0).astype(f32)
    label_row = jnp.pad(label_row[None, :], ((0, 7), (0, part.shape[1] - rows)))
    carried = jnp.concatenate([part, label_row], axis=0)
    carried = jnp.sum(lax.all_gather(carried, "col", axis=0), axis=0)
    carried = lax.all_gather(carried, "row", axis=0)

    all_p = ring_gather(sum_p.astype(bf16), "x", x, "z", z).reshape(count, units)
    all_q = ring_gather(sum_q.astype(bf16), "z", z, "x", x).transpose(1, 0, 2, 3).reshape(count, units)

    logits = carried[:, :rows].reshape(count, part.shape[1])
    every_label = carried[:, rows, :rows].reshape(count).astype(jnp.int32)
    exponent = jnp.exp(logits)
    partition = jnp.sum(exponent, axis=1, keepdims=True)
    classes = lax.broadcasted_iota(jnp.int32, logits.shape, 1)
    onehot = (every_label[:, None] == classes).astype(f32)
    costs = jnp.log(partition[:, 0]) - jnp.sum(logits * onehot, axis=1)
    token_loss = lax.dynamic_slice_in_dim(costs, col * own, own, 0)
    dlogits = (loss_scale * (exponent / partition - onehot)).astype(bf16)

    inner = jnp.zeros((count, width), f32)
    middle = []
    grads = []
    for sums, side, weight in (
        (all_p, down_head[:half], weight_p),
        (all_q, down_head[half:], weight_q),
    ):
        gate, up = sums[:, :half].astype(f32), sums[:, half:].astype(f32)
        dhidden = product_t(dlogits, side)
        sigmoid_gate = jax.nn.sigmoid(gate)
        activated = gate * sigmoid_gate
        hidden = (activated * up).astype(bf16)
        gate_delta = dhidden * up * sigmoid_gate * (1.0 + gate * (1.0 - sigmoid_gate))
        up_delta = dhidden * activated
        delta = jnp.concatenate([gate_delta.astype(bf16), up_delta.astype(bf16)], axis=1)
        inner += product_t(delta, weight)
        middle.append(t_product(hidden, dlogits))
        grads.append(t_product(every, delta))

    inner = inner.reshape(4, 2, own, width)
    kept_half = pick(inner, core, 1) + shift(pick(inner, 1 - core, 1).astype(bf16), "core", 1).astype(f32)
    mine = pick(kept_half, y)
    for step in (1, -1, 2):
        mine = mine + shift(pick(kept_half, y + step).astype(bf16), "y", step).astype(f32)
    dmixed = product_t(lax.dynamic_slice_in_dim(dlogits, col * own, own, 0), head_weight)
    tokens_grad = (dmixed.astype(bf16).astype(f32) + mine).astype(bf16)

    down_grad = kept_blocks(
        product_t(jnp.concatenate(middle, axis=0).astype(bf16), head_weight), down_mask
    ).astype(bf16)
    gate_grad = kept_blocks(
        jnp.concatenate([grads[0][:, :half], grads[1][:, :half]], axis=1), gate_mask
    ).astype(bf16)
    up_grad = kept_blocks(
        jnp.concatenate([grads[0][:, half:], grads[1][:, half:]], axis=1), up_mask
    ).astype(bf16)
    return (token_loss, tokens_grad, gate_grad, up_grad, down_grad)


def solution(mesh):
    placed = (
        P("col", "row"),
        P("row", "col"),
        P("row", "col"),
        P("col", "row"),
        P("row", "col"),
        P("row", "col"),
        P("col", "row"),
        P("row", None),
        P("col"),
    )
    return jax.shard_map(
        shards,
        mesh=mesh,
        in_specs=placed,
        out_specs=(P("col"), P("col", "row"), P("row", "col"), P("row", "col"), P("col", "row")),
        check_vma=False,
    )
```

```python
import jax
import jax.numpy as jnp
from jax import lax
from jax.experimental import pallas as pl
from jax.experimental.pallas import tpu as pltpu
from jax.sharding import PartitionSpec as P

loss_scale = 8.0
bf16 = jnp.bfloat16
f32 = jnp.float32
block = 64


def kept_blocks(weight, block_mask):
    height, breadth = weight.shape
    lanes = jnp.repeat(block_mask.astype(weight.dtype), breadth // block_mask.shape[1], axis=1)
    tall = weight.reshape(block_mask.shape[0], height // block_mask.shape[0], breadth)
    return (tall * lanes[:, None, :]).reshape(height, breadth)


def shift(value, line, step):
    if line == "x":
        pairs = [(r, (r // 4 + step) % 4 * 4 + r % 4) for r in range(16)]
        return lax.ppermute(value, "row", pairs)
    if line == "z":
        pairs = [(r, r // 4 * 4 + (r % 4 + step) % 4) for r in range(16)]
        return lax.ppermute(value, "row", pairs)
    if line == "y":
        pairs = [(c, (c // 2 + step) % 4 * 2 + c % 2) for c in range(8)]
        return lax.ppermute(value, "col", pairs)
    return lax.ppermute(value, "col", [(c, c ^ 1) for c in range(8)])


def pick(stack, at, axis=0):
    return lax.dynamic_index_in_dim(stack, at % stack.shape[axis], axis, keepdims=False)


def put(stack, value, at):
    return lax.dynamic_update_index_in_dim(stack, value, at % stack.shape[0], 0)


def product(left, right):
    return jnp.dot(left, right, preferred_element_type=f32)


def product_t(left, right):
    return lax.dot_general(left, right, (((1,), (1,)), ((), ())), preferred_element_type=f32)


def t_product(left, right):
    return lax.dot_general(left, right, (((0,), (0,)), ((), ())), preferred_element_type=f32)


def ring_sum(rows_of, weight, line, at, other, other_at):
    half = rows_of(at).shape[0] // 2
    far = product(rows_of(at + 2), weight).astype(bf16)
    far_up = shift(far[:half], line, 1)
    far_down = shift(far[half:], line, -1)
    up_rows, down_rows = rows_of(at + 1), rows_of(at - 1)
    up_late = shift(product(up_rows[half:], weight).astype(bf16), line, 1)
    down_late = shift(product(down_rows[:half], weight).astype(bf16), line, -1)
    up_first = shift((product(up_rows[:half], weight) + far_up.astype(f32)).astype(bf16), line, 1)
    down_first = shift((product(down_rows[half:], weight) + far_down.astype(f32)).astype(bf16), line, -1)
    from_below = jnp.concatenate([up_first, up_late], axis=0).astype(f32)
    from_above = jnp.concatenate([down_late, down_first], axis=0).astype(f32)
    mine = product(rows_of(at), weight) + from_below + from_above
    parts = mine.reshape(4, mine.shape[0] // 4, mine.shape[1])
    got = [
        shift(pick(parts, other_at + step).astype(bf16), other, step) for step in (1, -1, 2)
    ]
    total = pick(parts, other_at)
    for value in got:
        total = total + value.astype(f32)
    return total


def ring_chunk(mine, other, other_at):
    chunk = jnp.zeros((4,) + mine.shape, mine.dtype)
    chunk = put(chunk, mine, other_at)
    for step in (1, -1, 2):
        chunk = put(chunk, shift(mine, other, step), other_at - step)
    return chunk.reshape(4 * mine.shape[0], mine.shape[1])


def ring_spread(chunk, line):
    half = chunk.shape[0] // 2
    top, bottom = chunk[:half], chunk[half:]
    below_top = shift(top, line, 1)
    above_bottom = shift(bottom, line, -1)
    below_bottom = shift(bottom, line, 1)
    above_top = shift(top, line, -1)
    far_top = shift(below_top, line, 1)
    far_bottom = shift(above_bottom, line, -1)
    return (
        (0, (chunk,)),
        (-1, (below_top, below_bottom)),
        (1, (above_top, above_bottom)),
        (2, (far_top, far_bottom)),
    )


def back_kernel(count, *refs):
    _, *sums = refs[: 1 + count]
    dlogits_ref, side_ref, weight_ref, _, inner_in, middle_in, delta_ref, inner_ref, middle_ref = (
        refs[1 + count : 10 + count]
    )
    hidden_ref, flat_ref = refs[10 + count :]
    units = side_ref.shape[1]
    rows = flat_ref.shape[0]
    dlogits = dlogits_ref[...].reshape(rows, dlogits_ref.shape[-1])
    tall = 128
    for top in range(0, rows, tall):
        source = sums[top * count // rows]
        at = top if count == 1 else 0
        for left in range(0, units, 128):
            gate = source[at : at + tall, left : left + 128].astype(f32)
            up = source[at : at + tall, units + left : units + left + 128].astype(f32)
            dhidden = product(dlogits[top : top + tall], side_ref[:, left : left + 128])
            sigmoid_gate = 0.5 * jnp.tanh(0.5 * gate) + 0.5
            activated = gate * sigmoid_gate
            hidden_ref[top : top + tall, left : left + 128] = (activated * up).astype(bf16)
            gate_delta = dhidden * up * sigmoid_gate * (1.0 + gate * (1.0 - sigmoid_gate))
            flat_ref[top : top + tall, left : left + 128] = gate_delta.astype(bf16)
            flat_ref[top : top + tall, units + left : units + left + 128] = (
                dhidden * activated
            ).astype(bf16)
    delta_ref[...] = flat_ref[...].reshape(delta_ref.shape)
    inner_ref[...] = inner_in[...] + product_t(flat_ref[...], weight_ref[...]).reshape(inner_ref.shape)
    middle_ref[...] = middle_in[...] + t_product(dlogits, hidden_ref[...]).reshape(middle_ref.shape)


def back_step(part, at, pieces, dlogits, side, weight, delta, inner, middle):
    rows, wide = 256, weight.shape[1]
    classes, units = side.shape
    width = weight.shape[0]
    sub = rows // 4

    def place(columns, lead):
        if part == 0:
            shape, index = (1, 4, sub, columns), (lambda i, at: (at[0], 0, 0, 0))
        else:
            shape, index = (4, 1, sub, columns), (lambda i, at: (0, at[0], 0, 0))
        if lead:
            return pl.BlockSpec((1,) + shape, lambda i, at: (part,) + index(i, at))
        return pl.BlockSpec(shape, index)

    count = len(pieces)
    fixed = lambda shape: pl.BlockSpec(shape, lambda i, at: (0,) * len(shape))
    middle_spec = pl.BlockSpec((1, classes, units), lambda i, at: (part, 0, 0))
    return pl.pallas_call(
        lambda *refs: back_kernel(count, *refs),
        grid_spec=pltpu.PrefetchScalarGridSpec(
            num_scalar_prefetch=1,
            grid=(1,),
            in_specs=[fixed(piece.shape) for piece in pieces]
            + [
                place(classes, False),
                fixed(side.shape),
                fixed(weight.shape),
                pl.BlockSpec(memory_space=pl.ANY),
                place(width, False),
                middle_spec,
            ],
            out_specs=[place(wide, True), place(width, False), middle_spec],
            scratch_shapes=[pltpu.VMEM((rows, units), bf16), pltpu.VMEM((rows, wide), bf16)],
        ),
        out_shape=[
            jax.ShapeDtypeStruct(delta.shape, delta.dtype),
            jax.ShapeDtypeStruct(inner.shape, inner.dtype),
            jax.ShapeDtypeStruct(middle.shape, middle.dtype),
        ],
        input_output_aliases={count + 4: 0, count + 5: 1, count + 6: 2},
        compiler_params=pltpu.CompilerParams(vmem_limit_bytes=40 * 2**20),
        cost_estimate=pl.CostEstimate(
            flops=2 * rows * (wide * width + 2 * units * classes),
            bytes_accessed=4 * rows * wide + 2 * wide * width + 8 * rows * width,
            transcendentals=rows * units,
        ),
    )(jnp.reshape(at % 4, (1,)), *pieces, dlogits, side, weight, delta, inner, middle)


def grad_kernel(
    tokens_ref, delta_ref, middle_ref, head_ref, gate_lanes, up_lanes, down_lanes, gate_ref, up_ref, down_ref
):
    units = gate_ref.shape[1]
    blocks = gate_lanes.shape[0]
    for ref, lanes, left in ((gate_ref, gate_lanes, 0), (up_ref, up_lanes, units)):
        grad = product(tokens_ref[...], delta_ref[0, :, left : left + units])
        grad = grad.reshape(blocks, block, units) * lanes[...][:, None, :]
        ref[...] = grad.reshape(ref.shape).astype(bf16)
    down = lax.dot_general(
        middle_ref[0], head_ref[...], (((0,), (1,)), ((), ())), preferred_element_type=f32
    )
    down = down.reshape(down_lanes.shape[1], block, down.shape[1]) * down_lanes[0][:, None, :]
    down_ref[...] = down.reshape(down_ref.shape).astype(bf16)


def weight_grads(tokens_t, delta, middle, head, gate_mask, up_mask, down_mask):
    width, count = tokens_t.shape
    units = middle.shape[2]
    wide = 2 * units
    lanes = lambda mask, breadth: jnp.repeat(mask.astype(f32), breadth // mask.shape[1], axis=1)
    gate_lanes, up_lanes = lanes(gate_mask, wide), lanes(up_mask, wide)
    down_lanes = lanes(down_mask, width).reshape(2, -1, width)
    fixed = lambda shape: pl.BlockSpec(shape, lambda s: (0,) * len(shape))
    lead = lambda shape: pl.BlockSpec((1,) + shape[1:], lambda s: (s, 0, 0))
    side = lambda shape: pl.BlockSpec((shape[0], units), lambda s: (0, s))
    return pl.pallas_call(
        grad_kernel,
        grid=(2,),
        in_specs=[
            fixed(tokens_t.shape),
            lead(delta.shape),
            lead(middle.shape),
            fixed(head.shape),
            side(gate_lanes.shape),
            side(up_lanes.shape),
            lead(down_lanes.shape),
        ],
        out_specs=[side((width, wide)), side((width, wide)), pl.BlockSpec((units, width), lambda s: (s, 0))],
        out_shape=[
            jax.ShapeDtypeStruct((width, wide), bf16),
            jax.ShapeDtypeStruct((width, wide), bf16),
            jax.ShapeDtypeStruct((wide, width), bf16),
        ],
        compiler_params=pltpu.CompilerParams(vmem_limit_bytes=40 * 2**20),
        cost_estimate=pl.CostEstimate(
            flops=4 * count * wide * width, bytes_accessed=8 * count * wide, transcendentals=0
        ),
    )(tokens_t, delta, middle, head, gate_lanes, up_lanes, down_lanes)


def shards(
    tokens, gate_weight, up_weight, down_weight, gate_mask, up_mask, down_mask, head_weight, labels
):
    row, col = lax.axis_index("row"), lax.axis_index("col")
    x, z, y, core = row // 4, row % 4, col // 2, col % 2
    width = tokens.shape[1]
    own = tokens.shape[0]
    units = gate_weight.shape[1]
    half = units // 2
    count = own * 8
    rows = count // 16

    mates = put(jnp.zeros((4, own, width), bf16), tokens, y)
    for step in (1, -1, 2):
        mates = put(mates, shift(tokens, "y", step), y - step)
    others = shift(mates, "core", 1)
    first = core == 0
    every = jnp.stack([jnp.where(first, mates, others), jnp.where(first, others, mates)], axis=1)
    every = every.reshape(count, width)

    down_kept = kept_blocks(down_weight, down_mask)
    small = jnp.concatenate([product(down_kept, head_weight), product(tokens, head_weight)], axis=0)
    short = -small.shape[0] % 2048
    small = jnp.pad(small, ((0, short), (0, 0)))
    small = lax.psum_scatter(small, "row", scatter_dimension=0, tiled=True)
    small = lax.all_gather(small, "row", axis=0, tiled=True)
    down_head = small[:units].astype(bf16)
    token_head = small[units : units + own]

    gate_kept = kept_blocks(gate_weight, gate_mask)
    up_kept = kept_blocks(up_weight, up_mask)
    weight_p = jnp.concatenate([gate_kept[:, :half], up_kept[:, :half]], axis=1)
    weight_q = jnp.concatenate([gate_kept[:, half:], up_kept[:, half:]], axis=1)
    grid = every.reshape(4, 4, rows, width)
    sum_p = ring_sum(lambda j: pick(grid, j, 0).reshape(4 * rows, width), weight_p, "x", x, "z", z)
    sum_q = ring_sum(lambda j: pick(grid, j, 1).reshape(4 * rows, width), weight_q, "z", z, "x", x)

    part = jnp.zeros((rows, head_weight.shape[1]), f32)
    for sums, side in ((sum_p, down_head[:half]), (sum_q, down_head[half:])):
        gate, up = sums[:, :half], sums[:, half:]
        part += product((gate * jax.nn.sigmoid(gate) * up).astype(bf16), side)
    owner = col == row // 2
    start = row % 2 * rows
    part += jnp.where(owner, lax.dynamic_slice_in_dim(token_head, start, rows, 0), 0.0)
    label_row = jnp.where(owner, lax.dynamic_slice_in_dim(labels, start, rows, 0), 0).astype(f32)
    label_row = jnp.pad(label_row[None, :], ((0, 7), (0, part.shape[1] - rows)))
    carried = jnp.concatenate([part, label_row], axis=0)
    carried = jnp.sum(lax.all_gather(carried, "col", axis=0), axis=0)
    chunk_p = ring_chunk(sum_p.astype(bf16), "z", z)
    chunk_q = ring_chunk(sum_q.astype(bf16), "x", x)
    carried, chunk_p, chunk_q = lax.optimization_barrier((carried, chunk_p, chunk_q))
    spread_p, spread_q = ring_spread(chunk_p, "x"), ring_spread(chunk_q, "z")
    carried = lax.all_gather(carried, "row", axis=0)

    logits = carried[:, :rows].reshape(count, part.shape[1])
    every_label = carried[:, rows, :rows].reshape(count).astype(jnp.int32)
    exponent = jnp.exp(logits)
    partition = jnp.sum(exponent, axis=1, keepdims=True)
    classes = lax.broadcasted_iota(jnp.int32, logits.shape, 1)
    onehot = (every_label[:, None] == classes).astype(f32)
    costs = jnp.log(partition[:, 0]) - jnp.sum(logits * onehot, axis=1)
    token_loss = lax.dynamic_slice_in_dim(costs, col * own, own, 0)
    dlogits = (loss_scale * (exponent / partition - onehot)).astype(bf16)

    delta = jnp.zeros((2, 4, 4, rows, units), bf16)
    inner = jnp.zeros((4, 4, rows, width), f32)
    middle = jnp.zeros((2, dlogits.shape[1], half), f32)
    dlogits_grid = dlogits.reshape(4, 4, rows, -1)
    sides = jnp.transpose(down_head)
    for (away, piece_p), (_, piece_q) in zip(spread_p, spread_q):
        delta, inner, middle = back_step(
            0, x + away, piece_p, dlogits_grid, sides[:, :half], weight_p, delta, inner, middle
        )
        delta, inner, middle = back_step(
            1, z + away, piece_q, dlogits_grid, sides[:, half:], weight_q, delta, inner, middle
        )

    inner = inner.reshape(4, 2, own, width)
    kept_half = pick(inner, core, 1) + shift(pick(inner, 1 - core, 1).astype(bf16), "core", 1).astype(f32)
    mine = pick(kept_half, y)
    for step in (1, -1, 2):
        mine = mine + shift(pick(kept_half, y + step).astype(bf16), "y", step).astype(f32)
    dmixed = product_t(lax.dynamic_slice_in_dim(dlogits, col * own, own, 0), head_weight)
    tokens_grad = (dmixed.astype(bf16).astype(f32) + mine).astype(bf16)

    gate_grad, up_grad, down_grad = weight_grads(
        every.T,
        delta.reshape(2, count, units),
        middle.astype(bf16),
        head_weight,
        gate_mask,
        up_mask,
        down_mask,
    )
    return (token_loss, tokens_grad, gate_grad, up_grad, down_grad)


def solution(mesh):
    placed = (
        P("col", "row"),
        P("row", "col"),
        P("row", "col"),
        P("col", "row"),
        P("row", "col"),
        P("row", "col"),
        P("col", "row"),
        P("row", None),
        P("col"),
    )
    return jax.shard_map(
        shards,
        mesh=mesh,
        in_specs=placed,
        out_specs=(P("col"), P("col", "row"), P("row", "col"), P("row", "col"), P("col", "row")),
        check_vma=False,
    )
```

```python
import jax
import jax.numpy as jnp
from jax import lax
from jax.experimental import pallas as pl
from jax.experimental.pallas import tpu as pltpu
from jax.sharding import PartitionSpec as P

loss_scale = 8.0
bf16 = jnp.bfloat16
f32 = jnp.float32
block = 64


def kept_blocks(weight, block_mask):
    height, breadth = weight.shape
    lanes = jnp.repeat(block_mask.astype(weight.dtype), breadth // block_mask.shape[1], axis=1)
    tall = weight.reshape(block_mask.shape[0], height // block_mask.shape[0], breadth)
    return (tall * lanes[:, None, :]).reshape(height, breadth)


def shift(value, line, step):
    if line == "x":
        pairs = [(r, (r // 4 + step) % 4 * 4 + r % 4) for r in range(16)]
        return lax.ppermute(value, "row", pairs)
    if line == "z":
        pairs = [(r, r // 4 * 4 + (r % 4 + step) % 4) for r in range(16)]
        return lax.ppermute(value, "row", pairs)
    if line == "y":
        pairs = [(c, (c // 2 + step) % 4 * 2 + c % 2) for c in range(8)]
        return lax.ppermute(value, "col", pairs)
    return lax.ppermute(value, "col", [(c, c ^ 1) for c in range(8)])


def pick(stack, at, axis=0):
    at = at & (stack.shape[axis] - 1)
    return lax.dynamic_index_in_dim(stack, at, axis, keepdims=False, allow_negative_indices=False)


def put(stack, value, at):
    at = at & (stack.shape[0] - 1)
    return lax.dynamic_update_index_in_dim(stack, value, at, 0, allow_negative_indices=False)


def rows_at(stack, start, size):
    return lax.dynamic_slice_in_dim(stack, start, size, 0, allow_negative_indices=False)


def together(*values):
    return lax.optimization_barrier(values)


def to_all(value, axis, count):
    return lax.all_to_all(jnp.broadcast_to(value, (count,) + value.shape), axis, 0, 0, tiled=True)


def product(left, right):
    return jnp.dot(left, right, preferred_element_type=f32)


def product_t(left, right):
    return lax.dot_general(left, right, (((1,), (1,)), ((), ())), preferred_element_type=f32)


def t_product(left, right):
    return lax.dot_general(left, right, (((0,), (0,)), ((), ())), preferred_element_type=f32)


def back_kernel(count, *refs):
    _, *sums = refs[: 1 + count]
    dlogits_ref, side_ref, weight_ref, _, inner_in, middle_in, delta_ref, inner_ref, middle_ref = (
        refs[1 + count : 10 + count]
    )
    hidden_ref, flat_ref = refs[10 + count :]
    units = side_ref.shape[1]
    rows = flat_ref.shape[0]
    dlogits = dlogits_ref[...].reshape(rows, dlogits_ref.shape[-1])
    tall = 128
    for top in range(0, rows, tall):
        source = sums[top * count // rows]
        at = top if count == 1 else 0
        for left in range(0, units, 128):
            gate = source[at : at + tall, left : left + 128].astype(f32)
            up = source[at : at + tall, units + left : units + left + 128].astype(f32)
            dhidden = product(dlogits[top : top + tall], side_ref[:, left : left + 128])
            sigmoid_gate = 0.5 * jnp.tanh(0.5 * gate) + 0.5
            activated = gate * sigmoid_gate
            hidden_ref[top : top + tall, left : left + 128] = (activated * up).astype(bf16)
            gate_delta = dhidden * up * sigmoid_gate * (1.0 + gate * (1.0 - sigmoid_gate))
            flat_ref[top : top + tall, left : left + 128] = gate_delta.astype(bf16)
            flat_ref[top : top + tall, units + left : units + left + 128] = (
                dhidden * activated
            ).astype(bf16)
    delta_ref[...] = flat_ref[...].reshape(delta_ref.shape)
    inner_ref[...] = inner_in[...] + product_t(flat_ref[...], weight_ref[...]).reshape(inner_ref.shape)
    middle_ref[...] = middle_in[...] + t_product(dlogits, hidden_ref[...]).reshape(middle_ref.shape)


def back_step(part, at, pieces, dlogits, side, weight, delta, inner, middle):
    rows, wide = 256, weight.shape[1]
    classes, units = side.shape
    width = weight.shape[0]
    sub = rows // 4

    def place(columns, lead):
        if part == 0:
            shape, index = (1, 4, sub, columns), (lambda i, at: (at[0], 0, 0, 0))
        else:
            shape, index = (4, 1, sub, columns), (lambda i, at: (0, at[0], 0, 0))
        if lead:
            return pl.BlockSpec((1,) + shape, lambda i, at: (part,) + index(i, at))
        return pl.BlockSpec(shape, index)

    count = len(pieces)
    fixed = lambda shape: pl.BlockSpec(shape, lambda i, at: (0,) * len(shape))
    middle_spec = pl.BlockSpec((1, classes, units), lambda i, at: (part, 0, 0))
    return pl.pallas_call(
        lambda *refs: back_kernel(count, *refs),
        grid_spec=pltpu.PrefetchScalarGridSpec(
            num_scalar_prefetch=1,
            grid=(1,),
            in_specs=[fixed(piece.shape) for piece in pieces]
            + [
                place(classes, False),
                fixed(side.shape),
                fixed(weight.shape),
                pl.BlockSpec(memory_space=pl.ANY),
                place(width, False),
                middle_spec,
            ],
            out_specs=[place(wide, True), place(width, False), middle_spec],
            scratch_shapes=[pltpu.VMEM((rows, units), bf16), pltpu.VMEM((rows, wide), bf16)],
        ),
        out_shape=[
            jax.ShapeDtypeStruct(delta.shape, delta.dtype),
            jax.ShapeDtypeStruct(inner.shape, inner.dtype),
            jax.ShapeDtypeStruct(middle.shape, middle.dtype),
        ],
        input_output_aliases={count + 4: 0, count + 5: 1, count + 6: 2},
        compiler_params=pltpu.CompilerParams(vmem_limit_bytes=40 * 2**20),
        cost_estimate=pl.CostEstimate(
            flops=2 * rows * (wide * width + 2 * units * classes),
            bytes_accessed=4 * rows * wide + 2 * wide * width + 8 * rows * width,
            transcendentals=rows * units,
        ),
    )(jnp.reshape(at & 3, (1,)), *pieces, dlogits, side, weight, delta, inner, middle)


def grad_kernel(
    tokens_ref, delta_ref, middle_ref, head_ref, gate_lanes, up_lanes, down_lanes, gate_ref, up_ref, down_ref
):
    units = gate_ref.shape[1]
    blocks = gate_lanes.shape[0]
    for ref, lanes, left in ((gate_ref, gate_lanes, 0), (up_ref, up_lanes, units)):
        grad = product(tokens_ref[...], delta_ref[0, :, left : left + units])
        grad = grad.reshape(blocks, block, units) * lanes[...][:, None, :]
        ref[...] = grad.reshape(ref.shape).astype(bf16)
    down = lax.dot_general(
        middle_ref[0], head_ref[...], (((0,), (1,)), ((), ())), preferred_element_type=f32
    )
    down = down.reshape(down_lanes.shape[1], block, down.shape[1]) * down_lanes[0][:, None, :]
    down_ref[...] = down.reshape(down_ref.shape).astype(bf16)


def weight_grads(tokens_t, delta, middle, head, gate_mask, up_mask, down_mask):
    width, count = tokens_t.shape
    units = middle.shape[2]
    wide = 2 * units
    lanes = lambda mask, breadth: jnp.repeat(mask.astype(f32), breadth // mask.shape[1], axis=1)
    gate_lanes, up_lanes = lanes(gate_mask, wide), lanes(up_mask, wide)
    down_lanes = lanes(down_mask, width).reshape(2, -1, width)
    fixed = lambda shape: pl.BlockSpec(shape, lambda s: (0,) * len(shape))
    lead = lambda shape: pl.BlockSpec((1,) + shape[1:], lambda s: (s, 0, 0))
    side = lambda shape: pl.BlockSpec((shape[0], units), lambda s: (0, s))
    return pl.pallas_call(
        grad_kernel,
        grid=(2,),
        in_specs=[
            fixed(tokens_t.shape),
            lead(delta.shape),
            lead(middle.shape),
            fixed(head.shape),
            side(gate_lanes.shape),
            side(up_lanes.shape),
            lead(down_lanes.shape),
        ],
        out_specs=[side((width, wide)), side((width, wide)), pl.BlockSpec((units, width), lambda s: (s, 0))],
        out_shape=[
            jax.ShapeDtypeStruct((width, wide), bf16),
            jax.ShapeDtypeStruct((width, wide), bf16),
            jax.ShapeDtypeStruct((wide, width), bf16),
        ],
        compiler_params=pltpu.CompilerParams(vmem_limit_bytes=40 * 2**20),
        cost_estimate=pl.CostEstimate(
            flops=4 * count * wide * width, bytes_accessed=8 * count * wide, transcendentals=0
        ),
    )(tokens_t, delta, middle, head, gate_lanes, up_lanes, down_lanes)


def shards(
    tokens, gate_weight, up_weight, down_weight, gate_mask, up_mask, down_mask, head_weight, labels
):
    row, col = lax.axis_index("row"), lax.axis_index("col")
    x, z, y, core = row >> 2, row & 3, col >> 1, col & 1
    own, width = tokens.shape
    units = gate_weight.shape[1]
    half = units // 2
    count = own * 8
    rows = count // 16
    classes = head_weight.shape[1]

    mates = put(jnp.zeros((4, own, width), bf16), tokens, y)
    for step in (1, -1, 2):
        mates = put(mates, shift(tokens, "y", step), y - step)
    others = shift(mates, "core", 1)
    first = core == 0
    every = jnp.stack([jnp.where(first, mates, others), jnp.where(first, others, mates)], axis=1)
    every = every.reshape(count, width)
    grid = every.reshape(4, 4, rows, width)

    gate_kept = kept_blocks(gate_weight, gate_mask)
    up_kept = kept_blocks(up_weight, up_mask)
    weight_p = jnp.concatenate([gate_kept[:, :half], up_kept[:, :half]], axis=1)
    weight_q = jnp.concatenate([gate_kept[:, half:], up_kept[:, half:]], axis=1)

    p_rows = lambda away: pick(grid, x + away, 0).reshape(4 * rows, width)
    q_rows = lambda away: pick(grid, z + away, 1).reshape(4 * rows, width)
    mid = 2 * rows
    far_p = product(p_rows(2), weight_p).astype(bf16)
    far_q = product(q_rows(2), weight_q).astype(bf16)
    p_top, p_low, q_top, q_low = together(far_p[:mid], far_p[mid:], far_q[:mid], far_q[mid:])
    p_top, p_low = shift(p_top, "x", 1), shift(p_low, "x", -1)
    q_top, q_low = shift(q_top, "z", 1), shift(q_low, "z", -1)

    def joined(rows_of, weight, top, low):
        part = product(rows_of, weight)
        if top is not None:
            return jnp.concatenate([part[:mid] + top.astype(f32), part[mid:]], axis=0).astype(bf16)
        return jnp.concatenate([part[:mid], part[mid:] + low.astype(f32)], axis=0).astype(bf16)

    p_up, p_down, q_up, q_down, down_weight, down_mask_now = together(
        joined(p_rows(1), weight_p, p_top, None),
        joined(p_rows(-1), weight_p, None, p_low),
        joined(q_rows(1), weight_q, q_top, None),
        joined(q_rows(-1), weight_q, None, q_low),
        down_weight,
        down_mask,
    )
    p_up, p_down = shift(p_up, "x", 1), shift(p_down, "x", -1)
    q_up, q_down = shift(q_up, "z", 1), shift(q_down, "z", -1)

    down_kept = kept_blocks(down_weight, down_mask_now)

    def with_parts(down, token):
        high = lax.reduce_precision(token, 8, 7)
        low = (token - high).astype(bf16)
        return jnp.concatenate([down.astype(bf16), high.astype(bf16), low], axis=-2)

    small = with_parts(
        product(down_kept, head_weight).reshape(16, units // 16, classes),
        product(tokens, head_weight).reshape(16, own // 16, classes),
    )
    small = jnp.sum(lax.all_to_all(small, "row", 0, 0, tiled=True).astype(f32), axis=0)
    cut, last = units // 16, units // 16 + own // 16
    small = to_all(with_parts(small[:cut], small[cut:last] + small[last:]), "row", 16)
    down_head = small[:, :cut].reshape(units, classes)
    token_head = (small[:, cut:last].astype(f32) + small[:, last:].astype(f32)).reshape(own, classes)

    sum_p = product(p_rows(0), weight_p) + p_up.astype(f32) + p_down.astype(f32)
    sum_q = product(q_rows(0), weight_q) + q_up.astype(f32) + q_down.astype(f32)
    sum_p, sum_q = sum_p.reshape(4, rows, units), sum_q.reshape(4, rows, units)
    steps = (1, -1, 2)
    sends = together(
        *[pick(sum_p, z + step).astype(bf16) for step in steps],
        *[pick(sum_q, x + step).astype(bf16) for step in steps],
    )
    sum_p, sum_q = pick(sum_p, z), pick(sum_q, x)
    for step, send_p, send_q in zip(steps, sends[:3], sends[3:]):
        sum_p += shift(send_p, "z", step).astype(f32)
        sum_q += shift(send_q, "x", step).astype(f32)

    sum_p, sum_q, mine_p, mine_q = together(sum_p, sum_q, sum_p.astype(bf16), sum_q.astype(bf16))
    chunk_p = put(jnp.zeros((4, rows, units), bf16), mine_p, z)
    chunk_q = put(jnp.zeros((4, rows, units), bf16), mine_q, x)
    for step in steps:
        chunk_p = put(chunk_p, shift(mine_p, "z", step), z - step)
        chunk_q = put(chunk_q, shift(mine_q, "x", step), x - step)

    part = jnp.zeros((rows, classes), f32)
    for sums, side in ((sum_p, down_head[:half]), (sum_q, down_head[half:])):
        gate, up = sums[:, :half], sums[:, half:]
        part += product((gate * jax.nn.sigmoid(gate) * up).astype(bf16), side)
    owner = col == row >> 1
    start = (row & 1) * rows
    part += jnp.where(owner, rows_at(token_head, start, rows), 0.0)
    label_row = jnp.where(owner, rows_at(labels, start, rows), 0).astype(f32)
    label_row = jnp.pad(label_row[None, :], ((0, 7), (0, classes - rows)))
    carried = jnp.concatenate([part, label_row], axis=0)
    carried = jnp.sum(lax.all_gather(carried, "col", axis=0), axis=0)

    carried, chunk_p, chunk_q = together(carried, chunk_p, chunk_q)
    chunk_p, chunk_q = chunk_p.reshape(4 * rows, units), chunk_q.reshape(4 * rows, units)
    below_p, above_p = shift(chunk_p, "x", 1), shift(chunk_p, "x", -1)
    below_q, above_q = shift(chunk_q, "z", 1), shift(chunk_q, "z", -1)
    carried = to_all(carried, "row", 16)

    logits = carried[:, :rows].reshape(count, classes)
    every_label = carried[:, rows, :rows].reshape(count).astype(jnp.int32)
    exponent = jnp.exp(logits)
    partition = jnp.sum(exponent, axis=1, keepdims=True)
    places = lax.broadcasted_iota(jnp.int32, logits.shape, 1)
    onehot = (every_label[:, None] == places).astype(f32)
    costs = jnp.log(partition[:, 0]) - jnp.sum(logits * onehot, axis=1)
    token_loss = rows_at(costs, col * own, own)
    dlogits = (loss_scale * (exponent / partition - onehot)).astype(bf16)

    far_top_p, far_low_p, far_top_q, far_low_q, below_p, above_p, below_q, above_q = together(
        below_p[:mid], above_p[mid:], below_q[:mid], above_q[mid:], below_p, above_p, below_q, above_q
    )
    far_p = (shift(far_top_p, "x", 1), shift(far_low_p, "x", -1))
    far_q = (shift(far_top_q, "z", 1), shift(far_low_q, "z", -1))

    delta = jnp.zeros((2, 4, 4, rows, units), bf16)
    inner = jnp.zeros((4, 4, rows, width), f32)
    middle = jnp.zeros((2, classes, half), f32)
    dlogits_grid = dlogits.reshape(4, 4, rows, classes)
    sides = jnp.transpose(down_head)
    for away, piece_p, piece_q in (
        (0, (chunk_p,), (chunk_q,)),
        (-1, (below_p,), (below_q,)),
        (1, (above_p,), (above_q,)),
        (2, far_p, far_q),
    ):
        delta, inner, middle = back_step(
            0, x + away, piece_p, dlogits_grid, sides[:, :half], weight_p, delta, inner, middle
        )
        delta, inner, middle = back_step(
            1, z + away, piece_q, dlogits_grid, sides[:, half:], weight_q, delta, inner, middle
        )

    inner = inner.reshape(4, 2, own, width)
    kept_half = pick(inner, core, 1) + shift(pick(inner, 1 - core, 1).astype(bf16), "core", 1).astype(f32)
    mine = pick(kept_half, y)
    for step in (1, -1, 2):
        mine = mine + shift(pick(kept_half, y + step).astype(bf16), "y", step).astype(f32)
    dmixed = product_t(rows_at(dlogits, col * own, own), head_weight)
    tokens_grad = (dmixed.astype(bf16).astype(f32) + mine).astype(bf16)

    gate_grad, up_grad, down_grad = weight_grads(
        every.T,
        delta.reshape(2, count, units),
        middle.astype(bf16),
        head_weight,
        gate_mask,
        up_mask,
        down_mask,
    )
    return (token_loss, tokens_grad, gate_grad, up_grad, down_grad)


def solution(mesh):
    placed = (
        P("col", "row"),
        P("row", "col"),
        P("row", "col"),
        P("col", "row"),
        P("row", "col"),
        P("row", "col"),
        P("col", "row"),
        P("row", None),
        P("col"),
    )
    return jax.shard_map(
        shards,
        mesh=mesh,
        in_specs=placed,
        out_specs=(P("col"), P("col", "row"), P("row", "col"), P("row", "col"), P("col", "row")),
        check_vma=False,
    )
```

```python
import jax
import jax.numpy as jnp
from jax import lax
from jax.experimental import pallas as pl
from jax.experimental.pallas import tpu as pltpu
from jax.sharding import PartitionSpec as P

loss_scale = 8.0
bf16 = jnp.bfloat16
f32 = jnp.float32
block = 64


def kept_blocks(weight, block_mask):
    height, breadth = weight.shape
    lanes = jnp.repeat(block_mask.astype(weight.dtype), breadth // block_mask.shape[1], axis=1)
    tall = weight.reshape(block_mask.shape[0], height // block_mask.shape[0], breadth)
    return (tall * lanes[:, None, :]).reshape(height, breadth)


def shift(value, line, step):
    if line == "x":
        pairs = [(r, (r // 4 + step) % 4 * 4 + r % 4) for r in range(16)]
        return lax.ppermute(value, "row", pairs)
    if line == "z":
        pairs = [(r, r // 4 * 4 + (r % 4 + step) % 4) for r in range(16)]
        return lax.ppermute(value, "row", pairs)
    if line == "y":
        pairs = [(c, (c // 2 + step) % 4 * 2 + c % 2) for c in range(8)]
        return lax.ppermute(value, "col", pairs)
    return lax.ppermute(value, "col", [(c, c ^ 1) for c in range(8)])


def pick(stack, at, axis=0):
    at = at & (stack.shape[axis] - 1)
    return lax.dynamic_index_in_dim(stack, at, axis, keepdims=False, allow_negative_indices=False)


def put(stack, value, at):
    at = at & (stack.shape[0] - 1)
    return lax.dynamic_update_index_in_dim(stack, value, at, 0, allow_negative_indices=False)


def rows_at(stack, start, size):
    return lax.dynamic_slice_in_dim(stack, start, size, 0, allow_negative_indices=False)


def together(*values):
    return lax.optimization_barrier(values)


def to_all(value, axis, count):
    return lax.all_to_all(jnp.broadcast_to(value, (count,) + value.shape), axis, 0, 0, tiled=True)


def product(left, right):
    return jnp.dot(left, right, preferred_element_type=f32)


def product_t(left, right):
    return lax.dot_general(left, right, (((1,), (1,)), ((), ())), preferred_element_type=f32)


def t_product(left, right):
    return lax.dot_general(left, right, (((0,), (0,)), ((), ())), preferred_element_type=f32)


def back_kernel(part, count, at_ref, *refs):
    sums = refs[:count]
    dlogits_ref, side_ref, weight_ref, _, inner_in, middle_in, delta_ref, inner_ref, middle_ref = (
        refs[count : 9 + count]
    )
    dlogits_flat, hidden_flat, delta_flat = refs[9 + count :]
    units = side_ref.shape[1]
    rows = delta_flat.shape[0]
    sub = rows // 4
    places = [(0, at_ref[1 + k]) if part == 0 else (at_ref[1 + k], 0) for k in range(4)]
    for k in range(4):
        dlogits_flat[k * sub : (k + 1) * sub, :] = dlogits_ref[places[k]]
    tall = 128
    for top in range(0, rows, tall):
        source = sums[top * count // rows]
        at = top if count == 1 else 0
        for left in range(0, units, 128):
            gate = source[at : at + tall, left : left + 128].astype(f32)
            up = source[at : at + tall, units + left : units + left + 128].astype(f32)
            dhidden = product(dlogits_flat[top : top + tall, :], side_ref[:, left : left + 128])
            sigmoid_gate = 0.5 * jnp.tanh(0.5 * gate) + 0.5
            activated = gate * sigmoid_gate
            hidden_flat[top : top + tall, left : left + 128] = (activated * up).astype(bf16)
            gate_delta = dhidden * up * sigmoid_gate * (1.0 + gate * (1.0 - sigmoid_gate))
            delta_flat[top : top + tall, left : left + 128] = gate_delta.astype(bf16)
            delta_flat[top : top + tall, units + left : units + left + 128] = (
                dhidden * activated
            ).astype(bf16)
    inner = product_t(delta_flat[...], weight_ref[...])
    for k in range(4):
        span = slice(k * sub, (k + 1) * sub)
        delta_ref[places[k]] = delta_flat[span, :]
        inner_ref[places[k]] = inner_in[places[k]] + inner[span]
    middle_ref[...] = middle_in[...] + t_product(dlogits_flat[...], hidden_flat[...])


def back_step(part, at, pieces, dlogits, side, weight, delta, inner, middle):
    rows, wide = 256, weight.shape[1]
    classes, units = side.shape
    width = weight.shape[0]
    sub = rows // 4

    def place(columns):
        if part == 0:
            return pl.BlockSpec((1, 4, sub, columns), lambda i, at: (at[0], 0, 0, 0))
        return pl.BlockSpec((4, 1, sub, columns), lambda i, at: (0, at[0], 0, 0))

    count = len(pieces)
    fixed = lambda shape: pl.BlockSpec(shape, lambda i, at: (0,) * len(shape))
    return pl.pallas_call(
        lambda *refs: back_kernel(part, count, *refs),
        grid_spec=pltpu.PrefetchScalarGridSpec(
            num_scalar_prefetch=1,
            grid=(1,),
            in_specs=[fixed(piece.shape) for piece in pieces]
            + [
                place(classes),
                fixed(side.shape),
                fixed(weight.shape),
                pl.BlockSpec(memory_space=pl.ANY),
                place(width),
                fixed(middle.shape),
            ],
            out_specs=[place(wide), place(width), fixed(middle.shape)],
            scratch_shapes=[
                pltpu.VMEM((rows, classes), bf16),
                pltpu.VMEM((rows, units), bf16),
                pltpu.VMEM((rows, wide), bf16),
            ],
        ),
        out_shape=[
            jax.ShapeDtypeStruct(delta.shape, delta.dtype),
            jax.ShapeDtypeStruct(inner.shape, inner.dtype),
            jax.ShapeDtypeStruct(middle.shape, middle.dtype),
        ],
        input_output_aliases={count + 4: 0, count + 5: 1, count + 6: 2},
        compiler_params=pltpu.CompilerParams(vmem_limit_bytes=24 * 2**20),
        cost_estimate=pl.CostEstimate(
            flops=2 * rows * (wide * width + 2 * units * classes),
            bytes_accessed=4 * rows * wide + 2 * wide * width + 8 * rows * width,
            transcendentals=rows * units,
        ),
    )(at, *pieces, dlogits, side, weight, delta, inner, middle)


def grad_kernel(
    tokens_ref, delta_ref, middle_ref, head_ref, gate_lanes, up_lanes, down_lanes, *refs
):
    gate_ref, up_ref, down_ref = refs[-3:]
    units = gate_ref.shape[1]
    blocks = gate_lanes.shape[0]
    for ref, lanes, left in ((gate_ref, gate_lanes, 0), (up_ref, up_lanes, units)):
        grad = product(tokens_ref[...], delta_ref[:, left : left + units])
        grad = grad.reshape(blocks, block, units) * lanes[...][:, None, :]
        ref[...] = grad.reshape(ref.shape).astype(bf16)
    down = lax.dot_general(
        middle_ref[...].astype(bf16),
        head_ref[...],
        (((0,), (1,)), ((), ())),
        preferred_element_type=f32,
    )
    down = down.reshape(down_lanes.shape[1], block, down.shape[1]) * down_lanes[0][:, None, :]
    down_ref[...] = down.reshape(down_ref.shape).astype(bf16)


def weight_grads(part, before, tokens_t, delta, middle, head, gate_lanes, up_lanes, down_lanes):
    width, count = tokens_t.shape
    units = middle.shape[1]
    wide = 2 * units
    fixed = lambda shape: pl.BlockSpec(shape, lambda i: (0,) * len(shape))
    side = lambda height: pl.BlockSpec((height, units), lambda i: (0, part))
    return pl.pallas_call(
        grad_kernel,
        grid=(1,),
        in_specs=[
            fixed(tokens_t.shape),
            fixed(delta.shape),
            fixed(middle.shape),
            fixed(head.shape),
            side(gate_lanes.shape[0]),
            side(up_lanes.shape[0]),
            pl.BlockSpec((1,) + down_lanes.shape[1:], lambda i: (part, 0, 0)),
        ]
        + [pl.BlockSpec(memory_space=pl.ANY)] * len(before),
        out_specs=[side(width), side(width), pl.BlockSpec((units, width), lambda i: (part, 0))],
        out_shape=[
            jax.ShapeDtypeStruct((width, wide), bf16),
            jax.ShapeDtypeStruct((width, wide), bf16),
            jax.ShapeDtypeStruct((wide, width), bf16),
        ],
        input_output_aliases={7 + k: k for k in range(len(before))},
        compiler_params=pltpu.CompilerParams(vmem_limit_bytes=28 * 2**20),
        cost_estimate=pl.CostEstimate(
            flops=2 * count * wide * width, bytes_accessed=4 * count * wide, transcendentals=0
        ),
    )(tokens_t, delta, middle, head, gate_lanes, up_lanes, down_lanes, *before)


def shards(
    tokens, gate_weight, up_weight, down_weight, gate_mask, up_mask, down_mask, head_weight, labels
):
    row, col = lax.axis_index("row"), lax.axis_index("col")
    x, z, y, core = row >> 2, row & 3, col >> 1, col & 1
    own, width = tokens.shape
    units = gate_weight.shape[1]
    half = units // 2
    count = own * 8
    rows = count // 16
    classes = head_weight.shape[1]

    mates = put(jnp.zeros((4, own, width), bf16), tokens, y)
    for step in (1, -1, 2):
        mates = put(mates, shift(tokens, "y", step), y - step)
    others = shift(mates, "core", 1)
    first = core == 0
    every = jnp.stack([jnp.where(first, mates, others), jnp.where(first, others, mates)], axis=1)
    every = every.reshape(count, width)
    grid = every.reshape(4, 4, rows, width)

    gate_kept = kept_blocks(gate_weight, gate_mask)
    up_kept = kept_blocks(up_weight, up_mask)
    weight_p = jnp.concatenate([gate_kept[:, :half], up_kept[:, :half]], axis=1)
    weight_q = jnp.concatenate([gate_kept[:, half:], up_kept[:, half:]], axis=1)
    weight_p, weight_q = together(weight_p, weight_q)

    p_rows = lambda away: pick(grid, x + away, 0).reshape(4 * rows, width)
    q_rows = lambda away: pick(grid, z + away, 1).reshape(4 * rows, width)
    mid = 2 * rows
    far_p = product(p_rows(2), weight_p).astype(bf16)
    far_q = product(q_rows(2), weight_q).astype(bf16)
    p_top, p_low, q_top, q_low, down_weight, head_now, down_mask_now, grid = together(
        far_p[:mid], far_p[mid:], far_q[:mid], far_q[mid:], down_weight, head_weight, down_mask, grid
    )
    p_top, p_low = shift(p_top, "x", 1), shift(p_low, "x", -1)
    q_top, q_low = shift(q_top, "z", 1), shift(q_low, "z", -1)
    near = together(
        product(p_rows(1), weight_p),
        product(p_rows(-1), weight_p),
        product(q_rows(1), weight_q),
        product(q_rows(-1), weight_q),
    )
    above = lambda value: jnp.pad(value.astype(f32), ((0, mid), (0, 0)))
    under = lambda value: jnp.pad(value.astype(f32), ((mid, 0), (0, 0)))
    p_up, p_down, q_up, q_down = together(
        (near[0] + above(p_top)).astype(bf16),
        (near[1] + under(p_low)).astype(bf16),
        (near[2] + above(q_top)).astype(bf16),
        (near[3] + under(q_low)).astype(bf16),
    )
    p_up, p_down = shift(p_up, "x", 1), shift(p_down, "x", -1)
    q_up, q_down = shift(q_up, "z", 1), shift(q_down, "z", -1)

    down_kept = kept_blocks(down_weight, down_mask_now)

    def with_parts(down, token):
        high = lax.reduce_precision(token, 8, 7)
        low = (token - high).astype(bf16)
        return jnp.concatenate([down.astype(bf16), high.astype(bf16), low], axis=-2)

    small = with_parts(
        product(down_kept, head_now).reshape(16, units // 16, classes),
        product(tokens, head_now).reshape(16, own // 16, classes),
    )
    small = jnp.sum(lax.all_to_all(small, "row", 0, 0, tiled=True).astype(f32), axis=0)
    cut, last = units // 16, units // 16 + own // 16
    lanes = lambda mask, breadth: jnp.repeat(mask.astype(f32), breadth // mask.shape[1], axis=1)
    small, tokens_t, *masks = together(
        small,
        grid.reshape(count, width).T,
        lanes(gate_mask, units),
        lanes(up_mask, units),
        lanes(down_mask, width).reshape(2, -1, width),
    )
    small = to_all(with_parts(small[:cut], small[cut:last] + small[last:]), "row", 16)
    down_head = small[:, :cut].reshape(units, classes)
    token_head = (small[:, cut:last].astype(f32) + small[:, last:].astype(f32)).reshape(own, classes)

    own_p, own_q = together(product(p_rows(0), weight_p), product(q_rows(0), weight_q))

    def piece(values, at):
        total = 0.0
        for value in values:
            total = total + pick(value.reshape(4, rows, units), at).astype(f32)
        return total

    all_p, all_q = (own_p, p_up, p_down), (own_q, q_up, q_down)
    steps = (1, -1, 2)
    sends = together(
        *[piece(all_p, z + step).astype(bf16) for step in steps],
        *[piece(all_q, x + step).astype(bf16) for step in steps],
    )
    sum_p, sum_q = piece(all_p, z), piece(all_q, x)
    for step, send_p, send_q in zip(steps, sends[:3], sends[3:]):
        sum_p += shift(send_p, "z", step).astype(f32)
        sum_q += shift(send_q, "x", step).astype(f32)

    sum_p, sum_q, mine_p, mine_q, sides = together(
        sum_p, sum_q, sum_p.astype(bf16), sum_q.astype(bf16), jnp.transpose(down_head)
    )
    got_p = [mine_p] + [shift(mine_p, "z", step) for step in steps]
    got_q = [mine_q] + [shift(mine_q, "x", step) for step in steps]
    chunk_p, chunk_q = jnp.concatenate(got_p, axis=0), jnp.concatenate(got_q, axis=0)
    sum_p, sum_q, *_ = together(sum_p, sum_q, got_p[1], got_q[1])

    part = jnp.zeros((rows, classes), f32)
    for sums, side in ((sum_p, down_head[:half]), (sum_q, down_head[half:])):
        gate, up = sums[:, :half], sums[:, half:]
        part += product((gate * jax.nn.sigmoid(gate) * up).astype(bf16), side)
    owner = col == row >> 1
    start = (row & 1) * rows
    part += jnp.where(owner, rows_at(token_head, start, rows), 0.0)
    label_row = jnp.where(owner, rows_at(labels, start, rows), 0).astype(f32)
    label_row = jnp.pad(label_row[None, :], ((0, 7), (0, classes - rows)))
    carried = jnp.concatenate([part, label_row], axis=0)
    pairs = [[c, c + 1] for c in range(0, 8, 2)]
    carried = jnp.sum(lax.all_gather(carried, "col", axis=0, axis_index_groups=pairs), axis=0)
    carried = carried + sum(shift(carried, "y", step) for step in steps)

    chunk_p, chunk_q = together(chunk_p, chunk_q)
    below_p, above_p = shift(chunk_p, "x", 1), shift(chunk_p, "x", -1)
    below_q, above_q = shift(chunk_q, "z", 1), shift(chunk_q, "z", -1)
    carried = to_all(carried, "row", 16)

    logits = carried[:, :rows].reshape(count, classes)
    every_label = carried[:, rows, :rows].reshape(count).astype(jnp.int32)
    exponent = jnp.exp(logits)
    partition = jnp.sum(exponent, axis=1, keepdims=True)
    places = lax.broadcasted_iota(jnp.int32, logits.shape, 1)
    onehot = (every_label[:, None] == places).astype(f32)
    costs = jnp.log(partition[:, 0]) - jnp.sum(logits * onehot, axis=1)
    token_loss = rows_at(costs, col * own, own)
    dlogits = (loss_scale * (exponent / partition - onehot)).astype(bf16)

    far_p = (shift(below_p[:mid], "x", 1), shift(above_p[mid:], "x", -1))
    far_q = (shift(below_q[:mid], "z", 1), shift(above_q[mid:], "z", -1))

    delta_p = jnp.zeros((4, 4, rows, units), bf16)
    delta_q = jnp.zeros((4, 4, rows, units), bf16)
    inner = jnp.zeros((4, 4, rows, width), f32)
    middle_p = jnp.zeros((classes, half), f32)
    middle_q = jnp.zeros((classes, half), f32)
    dlogits_grid = dlogits.reshape(4, 4, rows, classes)
    spots = lambda at, away, other: jnp.stack([at + away, other, other - 1, other + 1, other + 2]) & 3
    for away, piece_p, piece_q in (
        (0, (chunk_p,), (chunk_q,)),
        (-1, (below_p,), (below_q,)),
        (1, (above_p,), (above_q,)),
        (2, far_p, far_q),
    ):
        delta_p, inner, middle_p = back_step(
            0, spots(x, away, z), piece_p, dlogits_grid, sides[:, :half], weight_p, delta_p, inner, middle_p
        )
        delta_q, inner, middle_q = back_step(
            1, spots(z, away, x), piece_q, dlogits_grid, sides[:, half:], weight_q, delta_q, inner, middle_q
        )

    inner = inner.reshape(4, 2, own, width)
    kept_half = pick(inner, core, 1) + shift(pick(inner, 1 - core, 1).astype(bf16), "core", 1).astype(f32)
    mine = pick(kept_half, y)
    for step in (1, -1, 2):
        mine = mine + shift(pick(kept_half, y + step).astype(bf16), "y", step).astype(f32)
    dmixed = product_t(rows_at(dlogits, col * own, own), head_weight)
    tokens_grad = (dmixed.astype(bf16).astype(f32) + mine).astype(bf16)

    grads = weight_grads(0, (), tokens_t, delta_p.reshape(count, units), middle_p, head_weight, *masks)
    gate_grad, up_grad, down_grad = weight_grads(
        1, grads, tokens_t, delta_q.reshape(count, units), middle_q, head_weight, *masks
    )
    return (token_loss, tokens_grad, gate_grad, up_grad, down_grad)


def solution(mesh):
    placed = (
        P("col", "row"),
        P("row", "col"),
        P("row", "col"),
        P("col", "row"),
        P("row", "col"),
        P("row", "col"),
        P("col", "row"),
        P("row", None),
        P("col"),
    )
    return jax.shard_map(
        shards,
        mesh=mesh,
        in_specs=placed,
        out_specs=(P("col"), P("col", "row"), P("row", "col"), P("row", "col"), P("col", "row")),
        check_vma=False,
    )
```

```python
import jax
import jax.numpy as jnp
from jax import lax
from jax.experimental import pallas as pl
from jax.experimental.pallas import tpu as pltpu
from jax.sharding import PartitionSpec as P

loss_scale = 8.0
bf16 = jnp.bfloat16
f32 = jnp.float32
block = 64


def kept_blocks(weight, block_mask):
    height, breadth = weight.shape
    lanes = jnp.repeat(block_mask.astype(weight.dtype), breadth // block_mask.shape[1], axis=1)
    tall = weight.reshape(block_mask.shape[0], height // block_mask.shape[0], breadth)
    return (tall * lanes[:, None, :]).reshape(height, breadth)


def shift(value, line, step):
    if line == "x":
        pairs = [(r, (r // 4 + step) % 4 * 4 + r % 4) for r in range(16)]
        return lax.ppermute(value, "row", pairs)
    if line == "z":
        pairs = [(r, r // 4 * 4 + (r % 4 + step) % 4) for r in range(16)]
        return lax.ppermute(value, "row", pairs)
    if line == "y":
        pairs = [(c, (c // 2 + step) % 4 * 2 + c % 2) for c in range(8)]
        return lax.ppermute(value, "col", pairs)
    return lax.ppermute(value, "col", [(c, c ^ 1) for c in range(8)])


def pick(stack, at, axis=0):
    at = at & (stack.shape[axis] - 1)
    return lax.dynamic_index_in_dim(stack, at, axis, keepdims=False, allow_negative_indices=False)


def put(stack, value, at):
    at = at & (stack.shape[0] - 1)
    return lax.dynamic_update_index_in_dim(stack, value, at, 0, allow_negative_indices=False)


def rows_at(stack, start, size):
    return lax.dynamic_slice_in_dim(stack, start, size, 0, allow_negative_indices=False)


def together(*values):
    return lax.optimization_barrier(values)


def to_all(value, axis, count):
    return lax.all_to_all(jnp.broadcast_to(value, (count,) + value.shape), axis, 0, 0, tiled=True)


def product(left, right):
    return jnp.dot(left, right, preferred_element_type=f32)


def product_t(left, right):
    return lax.dot_general(left, right, (((1,), (1,)), ((), ())), preferred_element_type=f32)


def t_product(left, right):
    return lax.dot_general(left, right, (((0,), (0,)), ((), ())), preferred_element_type=f32)


def spread_lanes(mask_ref, breadth):
    lanes = mask_ref.shape[-1]
    wide = lax.broadcasted_iota(jnp.int32, (lanes, breadth), 1)
    tall = lax.broadcasted_iota(jnp.int32, (lanes, breadth), 0) * block
    hit = jnp.where((wide >= tall) & (wide < tall + block), 1.0, 0.0)
    return product(mask_ref[...].astype(f32), hit)


def keep_kernel(gate_ref, up_ref, gate_mask, up_mask, p_ref, q_ref):
    units = gate_ref.shape[1]
    half = units // 2
    for ref, mask, left in ((gate_ref, gate_mask, 0), (up_ref, up_mask, half)):
        kept = spread_lanes(mask, units).astype(bf16)
        for k in range(mask.shape[0]):
            rows = slice(k * block, (k + 1) * block)
            value = ref[rows, :] * kept[k : k + 1, :]
            p_ref[rows, left : left + half] = value[:, :half]
            q_ref[rows, left : left + half] = value[:, half:]


def keep_weights(gate, up, gate_mask, up_mask):
    shape = jax.ShapeDtypeStruct(gate.shape, gate.dtype)
    tall = gate.shape[0]
    rows = pl.BlockSpec((tall, gate.shape[1]), lambda i: (i, 0))
    masks = pl.BlockSpec(gate_mask.shape, lambda i: (i, 0))
    return pl.pallas_call(
        keep_kernel,
        grid=(1,),
        in_specs=[rows, rows, masks, masks],
        out_specs=[rows, rows],
        out_shape=[shape, shape],
        compiler_params=pltpu.CompilerParams(vmem_limit_bytes=24 * 2**20),
        cost_estimate=pl.CostEstimate(
            flops=2 * gate.size, bytes_accessed=8 * gate.size, transcendentals=0
        ),
    )(gate, up, gate_mask, up_mask)


def loss_kernel(carried_ref, dlogits_ref, cost_ref):
    rows, classes = dlogits_ref.shape[1:]
    tall = lax.broadcasted_iota(jnp.int32, (rows, classes), 0)
    wide = lax.broadcasted_iota(jnp.int32, (rows, classes), 1)
    for k in range(dlogits_ref.shape[0]):
        logits = carried_ref[k, :rows, :]
        label_row = carried_ref[k, rows : rows + 1, :]
        label = jnp.sum(jnp.where(tall == wide, label_row, 0.0), axis=1, keepdims=True)
        onehot = jnp.where(label.astype(jnp.int32) == wide, 1.0, 0.0)
        exponent = jnp.exp(logits)
        partition = jnp.sum(exponent, axis=1, keepdims=True)
        cost = jnp.log(partition) - jnp.sum(logits * onehot, axis=1, keepdims=True)
        cost_ref[k : k + 1, :] = jnp.sum(jnp.where(tall == wide, cost, 0.0), axis=0, keepdims=True)
        dlogits_ref[k] = (loss_scale * (exponent / partition - onehot)).astype(bf16)


def losses(carried, rows):
    groups, _, classes = carried.shape
    whole = lambda shape: pl.BlockSpec(shape, lambda i: (0,) * len(shape))
    return pl.pallas_call(
        loss_kernel,
        grid=(1,),
        in_specs=[whole(carried.shape)],
        out_specs=[whole((groups, rows, classes)), whole((groups, classes))],
        out_shape=[
            jax.ShapeDtypeStruct((groups, rows, classes), bf16),
            jax.ShapeDtypeStruct((groups, classes), f32),
        ],
        compiler_params=pltpu.CompilerParams(vmem_limit_bytes=8 * 2**20),
        cost_estimate=pl.CostEstimate(
            flops=20 * carried.size, bytes_accessed=8 * carried.size, transcendentals=carried.size
        ),
    )(carried)


def back_kernel(parts, again, at_ref, *refs):
    count = len(parts)
    sums, refs = refs[: 2 * count], refs[2 * count :]
    dlogits_ref, sides, weights = refs[0], refs[1:3], refs[3:5]
    before = refs[5:9] if again else ()
    deltas, inner_ref, middle_ref, dlogits_flat, hidden_flat, delta_flat = (
        refs[-7:-5], *refs[-5:]
    )
    units = sides[0].shape[1]
    rows = delta_flat.shape[0]
    sub = rows // 4
    now = pl.program_id(0)

    @pl.when(now == 0)
    def _():
        inner_ref[...] = before[2][...] if again else jnp.zeros(inner_ref.shape, f32)
        middle_ref[...] = before[3][...] if again else jnp.zeros(middle_ref.shape, f32)

    def chunk(part, step, pair):
        chunk_at = at_ref[5 * step]
        others = [at_ref[5 * step + 1 + k] for k in range(4)]
        places = [(chunk_at, other) if part == 0 else (other, chunk_at) for other in others]
        local = [(0, other) if part == 0 else (other, 0) for other in others]
        for k in range(4):
            dlogits_flat[k * sub : (k + 1) * sub, :] = dlogits_ref[places[k]]
        tall = rows // 2
        for top, source in ((0, pair[0]), (tall, pair[1])):
            for left in range(0, units, 128):
                gate = source[:, left : left + 128].astype(f32)
                up = source[:, units + left : units + left + 128].astype(f32)
                dhidden = product(dlogits_flat[top : top + tall, :], sides[part][:, left : left + 128])
                sigmoid_gate = 0.5 * jnp.tanh(0.5 * gate) + 0.5
                activated = gate * sigmoid_gate
                hidden_flat[top : top + tall, left : left + 128] = (activated * up).astype(bf16)
                gate_delta = dhidden * up * sigmoid_gate * (1.0 + gate * (1.0 - sigmoid_gate))
                delta_flat[top : top + tall, left : left + 128] = gate_delta.astype(bf16)
                delta_flat[top : top + tall, units + left : units + left + 128] = (
                    dhidden * activated
                ).astype(bf16)
        inner = product_t(delta_flat[...], weights[part][...])
        for k in range(4):
            span = slice(k * sub, (k + 1) * sub)
            deltas[part][local[k]] = delta_flat[span, :]
            inner_ref[places[k]] = inner_ref[places[k]] + inner[span]
        middle_ref[part] = middle_ref[part] + t_product(dlogits_flat[...], hidden_flat[...])

    for step, part in enumerate(parts):
        pl.when(now == step)(
            lambda part=part, step=step: chunk(part, step, sums[2 * step : 2 * step + 2])
        )


def back_steps(chunks_p, chunks_q, spots, dlogits, sides, weights, before):
    pairs = [*chunks_p, *chunks_q]
    n_p, n_q = len(chunks_p), len(chunks_q)
    parts = (0,) * n_p + (1,) * n_q
    wide = pairs[0][0].shape[1]
    rows = 2 * pairs[0][0].shape[0]
    sub = rows // 4
    classes = dlogits.shape[-1]
    width, units = weights[0].shape[0], sides[0].shape[1]

    def whole(value, **mode):
        return pl.BlockSpec(value.shape, lambda i, at: (0,) * len(value.shape), **mode)

    once = dict(pipeline_mode=pl.Buffered(1))
    pieces = [half for pair in pairs for half in pair]
    shapes = [
        jax.ShapeDtypeStruct((4, 4, sub, wide), bf16),
        jax.ShapeDtypeStruct((4, 4, sub, wide), bf16),
        jax.ShapeDtypeStruct((4, 4, sub, width), f32),
        jax.ShapeDtypeStruct((2, classes, units), f32),
    ]
    fixed = [*pieces, dlogits, *sides, *weights]
    in_specs = [whole(value, **once) for value in fixed]
    aliases = {}
    if before:
        in_specs += [pl.BlockSpec(memory_space=pl.ANY)] * 2 + [whole(value, **once) for value in before[2:]]
        aliases = {1 + len(fixed) + k: k for k in range(4)}
    return pl.pallas_call(
        lambda *refs: back_kernel(parts, bool(before), *refs),
        grid_spec=pltpu.PrefetchScalarGridSpec(
            num_scalar_prefetch=1,
            grid=(n_p + n_q,),
            in_specs=in_specs,
            out_specs=[
                pl.BlockSpec(
                    (1, 4, sub, wide), lambda i, at: (at[5 * jnp.minimum(i, n_p - 1)], 0, 0, 0)
                ),
                pl.BlockSpec((4, 1, sub, wide), lambda i, at: (0, at[5 * jnp.maximum(i, n_p)], 0, 0)),
                whole(shapes[2]),
                whole(shapes[3]),
            ],
            scratch_shapes=[
                pltpu.VMEM((rows, classes), bf16),
                pltpu.VMEM((rows, units), bf16),
                pltpu.VMEM((rows, wide), bf16),
            ],
        ),
        out_shape=shapes,
        input_output_aliases=aliases,
        compiler_params=pltpu.CompilerParams(vmem_limit_bytes=36 * 2**20),
        cost_estimate=pl.CostEstimate(
            flops=2 * len(pairs) * rows * (wide * width + 2 * units * classes),
            bytes_accessed=len(pairs) * 4 * rows * wide + 4 * wide * width,
            transcendentals=len(pairs) * rows * units,
        ),
    )(spots, *fixed, *before)


def grad_kernel(tokens_ref, delta_ref, middle_ref, head_ref, gate_mask, up_mask, down_mask, *refs):
    gate_ref, up_ref, down_ref = refs[-3:]
    units = gate_ref.shape[1]
    for ref, mask, left in ((gate_ref, gate_mask, 0), (up_ref, up_mask, units)):
        grad = product(tokens_ref[...], delta_ref[:, left : left + units])
        lanes = spread_lanes(mask.at[0], units)
        grad = grad.reshape(lanes.shape[0], block, units) * lanes[:, None, :]
        ref[...] = grad.reshape(ref.shape).astype(bf16)
    down = lax.dot_general(
        middle_ref[0].astype(bf16), head_ref[...], (((0,), (1,)), ((), ())), preferred_element_type=f32
    )
    lanes = spread_lanes(down_mask.at[0], down.shape[1])
    down = down.reshape(lanes.shape[0], block, down.shape[1]) * lanes[:, None, :]
    down_ref[...] = down.reshape(down_ref.shape).astype(bf16)


def weight_grads(part, before, tokens_t, delta, middle, head, gate_mask, up_mask, down_mask):
    width, count = tokens_t.shape
    units = middle.shape[2]
    wide = 2 * units
    fixed = lambda value: pl.BlockSpec(value.shape, lambda i: (0,) * len(value.shape))
    lead = lambda value: pl.BlockSpec((1,) + value.shape[1:], lambda i: (part, 0, 0))
    side = pl.BlockSpec((width, units), lambda i: (0, part))
    return pl.pallas_call(
        grad_kernel,
        grid=(1,),
        in_specs=[
            fixed(tokens_t),
            fixed(delta),
            lead(middle),
            fixed(head),
            lead(gate_mask),
            lead(up_mask),
            lead(down_mask),
        ]
        + [pl.BlockSpec(memory_space=pl.ANY)] * len(before),
        out_specs=[side, side, pl.BlockSpec((units, width), lambda i: (part, 0))],
        out_shape=[
            jax.ShapeDtypeStruct((width, wide), bf16),
            jax.ShapeDtypeStruct((width, wide), bf16),
            jax.ShapeDtypeStruct((wide, width), bf16),
        ],
        input_output_aliases={7 + k: k for k in range(len(before))},
        compiler_params=pltpu.CompilerParams(vmem_limit_bytes=28 * 2**20),
        cost_estimate=pl.CostEstimate(
            flops=2 * count * wide * width, bytes_accessed=4 * count * wide, transcendentals=0
        ),
    )(tokens_t, delta, middle, head, gate_mask, up_mask, down_mask, *before)


def shards(
    tokens, gate_weight, up_weight, down_weight, gate_mask, up_mask, down_mask, head_weight, labels
):
    row, col = lax.axis_index("row"), lax.axis_index("col")
    x, z, y, core = row >> 2, row & 3, col >> 1, col & 1
    own, width = tokens.shape
    units = gate_weight.shape[1]
    half = units // 2
    count = own * 8
    rows = count // 16
    classes = head_weight.shape[1]

    mates = put(jnp.zeros((4, own, width), bf16), tokens, y)
    for step in (1, -1, 2):
        mates = put(mates, shift(tokens, "y", step), y - step)
    others = shift(mates, "core", 1)
    first = core == 0
    every = jnp.stack([jnp.where(first, mates, others), jnp.where(first, others, mates)], axis=1)
    every = every.reshape(count, width)
    grid = every.reshape(4, 4, rows, width)

    weight_p, weight_q = keep_weights(gate_weight, up_weight, gate_mask, up_mask)

    p_rows = lambda away: pick(grid, x + away, 0).reshape(4 * rows, width)
    q_rows = lambda away: pick(grid, z + away, 1).reshape(4 * rows, width)
    mid = 2 * rows
    far_p = product(p_rows(2), weight_p).astype(bf16)
    far_q = product(q_rows(2), weight_q).astype(bf16)
    p_top, p_low, q_top, q_low, down_weight, head_now, down_mask_now, grid = together(
        far_p[:mid], far_p[mid:], far_q[:mid], far_q[mid:], down_weight, head_weight, down_mask, grid
    )
    p_top, p_low = shift(p_top, "x", 1), shift(p_low, "x", -1)
    q_top, q_low = shift(q_top, "z", 1), shift(q_low, "z", -1)

    def joined(rows_of, weight, top, low):
        part = product(rows_of, weight)
        if top is not None:
            return jnp.concatenate([part[:mid] + top.astype(f32), part[mid:]], axis=0).astype(bf16)
        return jnp.concatenate([part[:mid], part[mid:] + low.astype(f32)], axis=0).astype(bf16)

    p_up, p_down = joined(p_rows(1), weight_p, p_top, None), joined(p_rows(-1), weight_p, None, p_low)
    q_up, q_down = joined(q_rows(1), weight_q, q_top, None), joined(q_rows(-1), weight_q, None, q_low)
    p_up, p_down = shift(p_up, "x", 1), shift(p_down, "x", -1)
    q_up, q_down = shift(q_up, "z", 1), shift(q_down, "z", -1)

    down_kept = kept_blocks(down_weight, down_mask_now)

    def with_parts(down, token):
        high = lax.reduce_precision(token, 8, 7)
        low = (token - high).astype(bf16)
        return jnp.concatenate([down.astype(bf16), high.astype(bf16), low], axis=-2)

    small = with_parts(
        product(down_kept, head_now).reshape(16, units // 16, classes),
        product(tokens, head_now).reshape(16, own // 16, classes),
    )
    small = jnp.sum(lax.all_to_all(small, "row", 0, 0, tiled=True).astype(f32), axis=0)
    cut, last = units // 16, units // 16 + own // 16
    small, tokens_t = together(small, grid.reshape(count, width).T)
    small = to_all(with_parts(small[:cut], small[cut:last] + small[last:]), "row", 16)
    down_head = small[:, :cut].reshape(units, classes)
    token_head = (small[:, cut:last].astype(f32) + small[:, last:].astype(f32)).reshape(own, classes)

    own_p, own_q = product(p_rows(0), weight_p), product(q_rows(0), weight_q)

    def piece(values, at):
        total = 0.0
        for value in values:
            total = total + pick(value.reshape(4, rows, units), at).astype(f32)
        return total

    all_p, all_q = (own_p, p_up, p_down), (own_q, q_up, q_down)
    steps = (1, -1, 2)
    sends = together(
        *[piece(all_p, z + step).astype(bf16) for step in steps],
        *[piece(all_q, x + step).astype(bf16) for step in steps],
    )
    sum_p, sum_q = piece(all_p, z), piece(all_q, x)
    for step, send_p, send_q in zip(steps, sends[:3], sends[3:]):
        sum_p += shift(send_p, "z", step).astype(f32)
        sum_q += shift(send_q, "x", step).astype(f32)

    sum_p, sum_q, mine_p, mine_q, sides = together(
        sum_p, sum_q, sum_p.astype(bf16), sum_q.astype(bf16), jnp.transpose(down_head)
    )
    got_p = [mine_p] + [shift(mine_p, "z", step) for step in steps]
    got_q = [mine_q] + [shift(mine_q, "x", step) for step in steps]
    in_halves = lambda got: (jnp.concatenate(got[:2], axis=0), jnp.concatenate(got[2:], axis=0))
    chunk_p, chunk_q = in_halves(got_p), in_halves(got_q)
    sum_p, sum_q, *_ = together(sum_p, sum_q, got_p[1], got_q[1])

    part = jnp.zeros((rows, classes), f32)
    for sums, side in ((sum_p, down_head[:half]), (sum_q, down_head[half:])):
        gate, up = sums[:, :half], sums[:, half:]
        part += product((gate * jax.nn.sigmoid(gate) * up).astype(bf16), side)
    owner = col == row >> 1
    start = (row & 1) * rows
    part += jnp.where(owner, rows_at(token_head, start, rows), 0.0)
    label_row = jnp.where(owner, rows_at(labels, start, rows), 0).astype(f32)
    label_row = jnp.pad(label_row[None, :], ((0, 7), (0, classes - rows)))
    carried = jnp.concatenate([part, label_row], axis=0)
    pairs = [[c, c + 1] for c in range(0, 8, 2)]
    carried = jnp.sum(lax.all_gather(carried, "col", axis=0, axis_index_groups=pairs), axis=0)
    carried = carried + sum(shift(carried, "y", step) for step in steps)

    p_top, q_top = together(chunk_p[0], chunk_q[0])
    p_low, q_low = together(chunk_p[1], chunk_q[1])
    below_p, below_q = [shift(p_top, "x", 1)], [shift(q_top, "z", 1)]
    above_p, above_q = [shift(p_top, "x", -1)], [shift(q_top, "z", -1)]
    above_p, above_q = above_p + [shift(p_low, "x", -1)], above_q + [shift(q_low, "z", -1)]
    below_p, below_q = below_p + [shift(p_low, "x", 1)], below_q + [shift(q_low, "z", 1)]
    far_p = [shift(below_p[0], "x", 1), shift(above_p[1], "x", -1)]
    far_q = [shift(below_q[0], "z", 1), shift(above_q[1], "z", -1)]
    carried = to_all(carried, "row", 16)

    dlogits_grid, costs = losses(carried, rows)
    token_loss = rows_at(costs, col * 2, 2)[:, :rows].reshape(own)
    dlogits = dlogits_grid.reshape(count, classes)
    dlogits_grid = dlogits_grid.reshape(4, 4, rows, classes)

    def spots(at, other, aways):
        return [jnp.stack([at + away, other, other - 1, other + 1, other + 2]) & 3 for away in aways]

    first_spots = jnp.concatenate(spots(x, z, (0, -1, 1)) + spots(z, x, (0, -1, 1)))
    last_spots = jnp.concatenate(spots(x, z, (2,)) + spots(z, x, (2,)))
    halves = (sides[:, :half], sides[:, half:])
    weights = (weight_p, weight_q)
    state = back_steps(
        (chunk_p, below_p, above_p), (chunk_q, below_q, above_q), first_spots, dlogits_grid, halves, weights, ()
    )
    delta_p, delta_q, inner, middle = back_steps(
        (far_p,), (far_q,), last_spots, dlogits_grid, halves, weights, state
    )

    inner = inner.reshape(4, 2, own, width)
    kept_half = pick(inner, core, 1) + shift(pick(inner, 1 - core, 1).astype(bf16), "core", 1).astype(f32)
    mine = pick(kept_half, y)
    for step in (1, -1, 2):
        mine = mine + shift(pick(kept_half, y + step).astype(bf16), "y", step).astype(f32)
    dmixed = product_t(rows_at(dlogits, col * own, own), head_weight)
    tokens_grad = (dmixed.astype(bf16).astype(f32) + mine).astype(bf16)

    by_side = lambda mask: jnp.stack(jnp.split(mask, 2, axis=1))
    masks = (by_side(gate_mask), by_side(up_mask), jnp.stack(jnp.split(down_mask, 2, axis=0)))
    grads = weight_grads(0, (), tokens_t, delta_p.reshape(count, units), middle, head_weight, *masks)
    gate_grad, up_grad, down_grad = weight_grads(
        1, grads, tokens_t, delta_q.reshape(count, units), middle, head_weight, *masks
    )
    return (token_loss, tokens_grad, gate_grad, up_grad, down_grad)


def solution(mesh):
    placed = (
        P("col", "row"),
        P("row", "col"),
        P("row", "col"),
        P("col", "row"),
        P("row", "col"),
        P("row", "col"),
        P("col", "row"),
        P("row", None),
        P("col"),
    )
    return jax.shard_map(
        shards,
        mesh=mesh,
        in_specs=placed,
        out_specs=(P("col"), P("col", "row"), P("row", "col"), P("row", "col"), P("col", "row")),
        check_vma=False,
    )
```

```python
import jax
import jax.numpy as jnp
from jax import lax
from jax.experimental import pallas as pl
from jax.experimental.pallas import tpu as pltpu
from jax.sharding import PartitionSpec as P

loss_scale = 8.0
bf16 = jnp.bfloat16
f32 = jnp.float32
block = 64


def kept_blocks(weight, block_mask):
    height, breadth = weight.shape
    lanes = jnp.repeat(block_mask.astype(weight.dtype), breadth // block_mask.shape[1], axis=1)
    tall = weight.reshape(block_mask.shape[0], height // block_mask.shape[0], breadth)
    return (tall * lanes[:, None, :]).reshape(height, breadth)


def shift(value, line, step):
    if line == "x":
        pairs = [(r, (r // 4 + step) % 4 * 4 + r % 4) for r in range(16)]
        return lax.ppermute(value, "row", pairs)
    if line == "z":
        pairs = [(r, r // 4 * 4 + (r % 4 + step) % 4) for r in range(16)]
        return lax.ppermute(value, "row", pairs)
    if line == "y":
        pairs = [(c, (c // 2 + step) % 4 * 2 + c % 2) for c in range(8)]
        return lax.ppermute(value, "col", pairs)
    return lax.ppermute(value, "col", [(c, c ^ 1) for c in range(8)])


def pick(stack, at, axis=0):
    at = at & (stack.shape[axis] - 1)
    return lax.dynamic_index_in_dim(stack, at, axis, keepdims=False, allow_negative_indices=False)


def put(stack, value, at):
    at = at & (stack.shape[0] - 1)
    return lax.dynamic_update_index_in_dim(stack, value, at, 0, allow_negative_indices=False)


def rows_at(stack, start, size):
    return lax.dynamic_slice_in_dim(stack, start, size, 0, allow_negative_indices=False)


def together(*values):
    return lax.optimization_barrier(values)


def to_all(value, axis, count):
    return lax.all_to_all(jnp.broadcast_to(value, (count,) + value.shape), axis, 0, 0, tiled=True)


def product(left, right):
    return jnp.dot(left, right, preferred_element_type=f32)


def product_t(left, right):
    return lax.dot_general(left, right, (((1,), (1,)), ((), ())), preferred_element_type=f32)


def t_product(left, right):
    return lax.dot_general(left, right, (((0,), (0,)), ((), ())), preferred_element_type=f32)


def spread_lanes(mask_ref, breadth):
    lanes = mask_ref.shape[-1]
    wide = lax.broadcasted_iota(jnp.int32, (lanes, breadth), 1)
    tall = lax.broadcasted_iota(jnp.int32, (lanes, breadth), 0) * block
    hit = jnp.where((wide >= tall) & (wide < tall + block), 1.0, 0.0)
    return product(mask_ref[...].astype(f32), hit)


def keep_kernel(gate_ref, up_ref, gate_mask, up_mask, p_ref, q_ref):
    units = gate_ref.shape[1]
    half = units // 2
    for ref, mask, left in ((gate_ref, gate_mask, 0), (up_ref, up_mask, half)):
        kept = spread_lanes(mask, units).astype(bf16)
        for k in range(mask.shape[0]):
            rows = slice(k * block, (k + 1) * block)
            value = ref[rows, :] * kept[k : k + 1, :]
            p_ref[rows, left : left + half] = value[:, :half]
            q_ref[rows, left : left + half] = value[:, half:]


def keep_weights(gate, up, gate_mask, up_mask):
    shape = jax.ShapeDtypeStruct(gate.shape, gate.dtype)
    tall = gate.shape[0]
    rows = pl.BlockSpec((tall, gate.shape[1]), lambda i: (i, 0))
    masks = pl.BlockSpec(gate_mask.shape, lambda i: (i, 0))
    return pl.pallas_call(
        keep_kernel,
        grid=(1,),
        in_specs=[rows, rows, masks, masks],
        out_specs=[rows, rows],
        out_shape=[shape, shape],
        compiler_params=pltpu.CompilerParams(vmem_limit_bytes=24 * 2**20),
        cost_estimate=pl.CostEstimate(
            flops=2 * gate.size, bytes_accessed=8 * gate.size, transcendentals=0
        ),
    )(gate, up, gate_mask, up_mask)


def join_kernel(low, rows_ref, weight_ref, got_ref, out_ref):
    half = got_ref.shape[0]
    for k in range(2):
        span = slice(k * half, (k + 1) * half)
        part = product(rows_ref[span, :], weight_ref[...])
        if low == bool(k):
            part = part + got_ref[...].astype(f32)
        out_ref[span, :] = part.astype(bf16)


def join(rows, weight, got, low):
    whole = lambda value: pl.BlockSpec(value.shape, lambda i: (0, 0))
    shape = jax.ShapeDtypeStruct((rows.shape[0], weight.shape[1]), bf16)
    return pl.pallas_call(
        lambda *refs: join_kernel(low, *refs),
        grid=(1,),
        in_specs=[whole(rows), whole(weight), whole(got)],
        out_specs=whole(shape),
        out_shape=shape,
        compiler_params=pltpu.CompilerParams(vmem_limit_bytes=16 * 2**20),
        cost_estimate=pl.CostEstimate(
            flops=2 * rows.shape[0] * weight.size, bytes_accessed=2 * weight.size, transcendentals=0
        ),
    )(rows, weight, got)


def own_kernel(at_ref, rows_ref, weight_ref, up_ref, down_ref, *refs):
    *outs, mine_ref, parts_ref = refs
    sub = mine_ref.shape[0]
    half = 2 * sub
    for k in range(2):
        span = slice(k * half, (k + 1) * half)
        part = product(rows_ref[span, :], weight_ref[...])
        part = part + up_ref[span, :].astype(f32) + down_ref[span, :].astype(f32)
        parts_ref[2 * k : 2 * k + 2] = part.reshape(2, sub, part.shape[1])
    mine_ref[...] = parts_ref[at_ref[0]]
    for k, out in enumerate(outs):
        out[...] = parts_ref[at_ref[1 + k]].astype(bf16)


def own_pieces(rows, weight, up, down, at, steps):
    sub, wide = rows.shape[0] // 4, weight.shape[1]
    spots = jnp.stack([at] + [at + step for step in steps]) & 3
    whole = lambda value: pl.BlockSpec(value.shape, lambda i, at: (0, 0))
    shapes = [jax.ShapeDtypeStruct((sub, wide), bf16)] * len(steps)
    shapes += [jax.ShapeDtypeStruct((sub, wide), f32)]
    *sends, mine = pl.pallas_call(
        own_kernel,
        grid_spec=pltpu.PrefetchScalarGridSpec(
            num_scalar_prefetch=1,
            grid=(1,),
            in_specs=[whole(value) for value in (rows, weight, up, down)],
            out_specs=[whole(shape) for shape in shapes],
            scratch_shapes=[pltpu.VMEM((4, sub, wide), f32)],
        ),
        out_shape=shapes,
        compiler_params=pltpu.CompilerParams(vmem_limit_bytes=20 * 2**20),
        cost_estimate=pl.CostEstimate(
            flops=2 * rows.shape[0] * weight.size, bytes_accessed=4 * weight.size, transcendentals=0
        ),
    )(spots, rows, weight, up, down)
    return sends, mine


def loss_kernel(carried_ref, dlogits_ref, cost_ref):
    rows, classes = dlogits_ref.shape[1:]
    tall = lax.broadcasted_iota(jnp.int32, (rows, classes), 0)
    wide = lax.broadcasted_iota(jnp.int32, (rows, classes), 1)
    for k in range(dlogits_ref.shape[0]):
        logits = carried_ref[k, :rows, :]
        label_row = carried_ref[k, rows : rows + 1, :]
        label = jnp.sum(jnp.where(tall == wide, label_row, 0.0), axis=1, keepdims=True)
        onehot = jnp.where(label.astype(jnp.int32) == wide, 1.0, 0.0)
        exponent = jnp.exp(logits)
        partition = jnp.sum(exponent, axis=1, keepdims=True)
        cost = jnp.log(partition) - jnp.sum(logits * onehot, axis=1, keepdims=True)
        cost_ref[k : k + 1, :] = jnp.sum(jnp.where(tall == wide, cost, 0.0), axis=0, keepdims=True)
        dlogits_ref[k] = (loss_scale * (exponent / partition - onehot)).astype(bf16)


def losses(carried, rows):
    groups, _, classes = carried.shape
    whole = lambda shape: pl.BlockSpec(shape, lambda i: (0,) * len(shape))
    return pl.pallas_call(
        loss_kernel,
        grid=(1,),
        in_specs=[whole(carried.shape)],
        out_specs=[whole((groups, rows, classes)), whole((groups, classes))],
        out_shape=[
            jax.ShapeDtypeStruct((groups, rows, classes), bf16),
            jax.ShapeDtypeStruct((groups, classes), f32),
        ],
        compiler_params=pltpu.CompilerParams(vmem_limit_bytes=8 * 2**20),
        cost_estimate=pl.CostEstimate(
            flops=20 * carried.size, bytes_accessed=8 * carried.size, transcendentals=carried.size
        ),
    )(carried)


def back_kernel(parts, again, at_ref, *refs):
    count = len(parts)
    sums, refs = refs[: 2 * count], refs[2 * count :]
    dlogits_ref, sides, weights = refs[0], refs[1:3], refs[3:5]
    before = refs[5:9] if again else ()
    deltas, inner_ref, middle_ref, dlogits_flat, hidden_flat, delta_flat = (
        refs[-7:-5], *refs[-5:]
    )
    units = sides[0].shape[1]
    rows = delta_flat.shape[0]
    sub = rows // 4
    now = pl.program_id(0)

    @pl.when(now == 0)
    def _():
        inner_ref[...] = before[2][...] if again else jnp.zeros(inner_ref.shape, f32)
        middle_ref[...] = before[3][...] if again else jnp.zeros(middle_ref.shape, f32)

    def chunk(part, step, pair):
        chunk_at = at_ref[5 * step]
        others = [at_ref[5 * step + 1 + k] for k in range(4)]
        places = [(chunk_at, other) if part == 0 else (other, chunk_at) for other in others]
        local = [(0, other) if part == 0 else (other, 0) for other in others]
        for k in range(4):
            dlogits_flat[k * sub : (k + 1) * sub, :] = dlogits_ref[places[k]]
        tall = rows // 2
        for top, source in ((0, pair[0]), (tall, pair[1])):
            for left in range(0, units, 128):
                gate = source[:, left : left + 128].astype(f32)
                up = source[:, units + left : units + left + 128].astype(f32)
                dhidden = product(dlogits_flat[top : top + tall, :], sides[part][:, left : left + 128])
                sigmoid_gate = 0.5 * jnp.tanh(0.5 * gate) + 0.5
                activated = gate * sigmoid_gate
                hidden_flat[top : top + tall, left : left + 128] = (activated * up).astype(bf16)
                gate_delta = dhidden * up * sigmoid_gate * (1.0 + gate * (1.0 - sigmoid_gate))
                delta_flat[top : top + tall, left : left + 128] = gate_delta.astype(bf16)
                delta_flat[top : top + tall, units + left : units + left + 128] = (
                    dhidden * activated
                ).astype(bf16)
        inner = product_t(delta_flat[...], weights[part][...])
        for k in range(4):
            span = slice(k * sub, (k + 1) * sub)
            deltas[part][local[k]] = delta_flat[span, :]
            inner_ref[places[k]] = inner_ref[places[k]] + inner[span]
        middle_ref[part] = middle_ref[part] + t_product(dlogits_flat[...], hidden_flat[...])

    for step, part in enumerate(parts):
        pl.when(now == step)(
            lambda part=part, step=step: chunk(part, step, sums[2 * step : 2 * step + 2])
        )


def back_steps(chunks_p, chunks_q, spots, dlogits, sides, weights, before):
    pairs = [*chunks_p, *chunks_q]
    n_p, n_q = len(chunks_p), len(chunks_q)
    parts = (0,) * n_p + (1,) * n_q
    wide = pairs[0][0].shape[1]
    rows = 2 * pairs[0][0].shape[0]
    sub = rows // 4
    classes = dlogits.shape[-1]
    width, units = weights[0].shape[0], sides[0].shape[1]

    def whole(value, **mode):
        return pl.BlockSpec(value.shape, lambda i, at: (0,) * len(value.shape), **mode)

    once = dict(pipeline_mode=pl.Buffered(1))
    pieces = [half for pair in pairs for half in pair]
    shapes = [
        pltpu.HBM((4, 4, sub, wide), bf16),
        pltpu.HBM((4, 4, sub, wide), bf16),
        pltpu.HBM((4, 4, sub, width), f32),
        pltpu.HBM((2, classes, units), f32),
    ]
    fixed = [*pieces, dlogits, *sides, *weights]
    in_specs = [whole(value, **once) for value in fixed]
    aliases = {}
    if before:
        in_specs += [pl.BlockSpec(memory_space=pl.ANY)] * 2 + [whole(value, **once) for value in before[2:]]
        aliases = {1 + len(fixed) + k: k for k in range(4)}
    return pl.pallas_call(
        lambda *refs: back_kernel(parts, bool(before), *refs),
        grid_spec=pltpu.PrefetchScalarGridSpec(
            num_scalar_prefetch=1,
            grid=(n_p + n_q,),
            in_specs=in_specs,
            out_specs=[
                pl.BlockSpec(
                    (1, 4, sub, wide), lambda i, at: (at[5 * jnp.minimum(i, n_p - 1)], 0, 0, 0)
                ),
                pl.BlockSpec((4, 1, sub, wide), lambda i, at: (0, at[5 * jnp.maximum(i, n_p)], 0, 0)),
                whole(shapes[2]),
                whole(shapes[3]),
            ],
            scratch_shapes=[
                pltpu.VMEM((rows, classes), bf16),
                pltpu.VMEM((rows, units), bf16),
                pltpu.VMEM((rows, wide), bf16),
            ],
        ),
        out_shape=shapes,
        input_output_aliases=aliases,
        compiler_params=pltpu.CompilerParams(vmem_limit_bytes=36 * 2**20),
        cost_estimate=pl.CostEstimate(
            flops=2 * len(pairs) * rows * (wide * width + 2 * units * classes),
            bytes_accessed=len(pairs) * 4 * rows * wide + 4 * wide * width,
            transcendentals=len(pairs) * rows * units,
        ),
    )(spots, *fixed, *before)


def grad_kernel(tokens_ref, delta_ref, middle_ref, head_ref, gate_mask, up_mask, down_mask, *refs):
    gate_ref, up_ref, down_ref = refs[-3:]
    units = gate_ref.shape[1]
    for ref, mask, left in ((gate_ref, gate_mask, 0), (up_ref, up_mask, units)):
        grad = product(tokens_ref[...], delta_ref[:, left : left + units])
        lanes = spread_lanes(mask.at[0], units)
        grad = grad.reshape(lanes.shape[0], block, units) * lanes[:, None, :]
        ref[...] = grad.reshape(ref.shape).astype(bf16)
    down = lax.dot_general(
        middle_ref[0].astype(bf16), head_ref[...], (((0,), (1,)), ((), ())), preferred_element_type=f32
    )
    lanes = spread_lanes(down_mask.at[0], down.shape[1])
    down = down.reshape(lanes.shape[0], block, down.shape[1]) * lanes[:, None, :]
    down_ref[...] = down.reshape(down_ref.shape).astype(bf16)


def weight_grads(part, before, tokens_t, delta, middle, head, gate_mask, up_mask, down_mask):
    width, count = tokens_t.shape
    units = middle.shape[2]
    wide = 2 * units
    fixed = lambda value: pl.BlockSpec(value.shape, lambda i: (0,) * len(value.shape))
    lead = lambda value: pl.BlockSpec((1,) + value.shape[1:], lambda i: (part, 0, 0))
    side = pl.BlockSpec((width, units), lambda i: (0, part))
    return pl.pallas_call(
        grad_kernel,
        grid=(1,),
        in_specs=[
            fixed(tokens_t),
            fixed(delta),
            lead(middle),
            fixed(head),
            lead(gate_mask),
            lead(up_mask),
            lead(down_mask),
        ]
        + [pl.BlockSpec(memory_space=pl.ANY)] * len(before),
        out_specs=[side, side, pl.BlockSpec((units, width), lambda i: (part, 0))],
        out_shape=[
            jax.ShapeDtypeStruct((width, wide), bf16),
            jax.ShapeDtypeStruct((width, wide), bf16),
            jax.ShapeDtypeStruct((wide, width), bf16),
        ],
        input_output_aliases={7 + k: k for k in range(len(before))},
        compiler_params=pltpu.CompilerParams(vmem_limit_bytes=28 * 2**20),
        cost_estimate=pl.CostEstimate(
            flops=2 * count * wide * width, bytes_accessed=4 * count * wide, transcendentals=0
        ),
    )(tokens_t, delta, middle, head, gate_mask, up_mask, down_mask, *before)


def shards(
    tokens, gate_weight, up_weight, down_weight, gate_mask, up_mask, down_mask, head_weight, labels
):
    row, col = lax.axis_index("row"), lax.axis_index("col")
    x, z, y, core = row >> 2, row & 3, col >> 1, col & 1
    own, width = tokens.shape
    units = gate_weight.shape[1]
    half = units // 2
    count = own * 8
    rows = count // 16
    classes = head_weight.shape[1]

    mates = put(jnp.zeros((4, own, width), bf16), tokens, y)
    for step in (1, -1, 2):
        mates = put(mates, shift(tokens, "y", step), y - step)
    others = shift(mates, "core", 1)
    first = core == 0
    every = jnp.stack([jnp.where(first, mates, others), jnp.where(first, others, mates)], axis=1)
    every = every.reshape(count, width)
    grid = every.reshape(4, 4, rows, width)

    weight_p, weight_q = keep_weights(gate_weight, up_weight, gate_mask, up_mask)

    p_rows = lambda away: pick(grid, x + away, 0).reshape(4 * rows, width)
    q_rows = lambda away: pick(grid, z + away, 1).reshape(4 * rows, width)
    mid = 2 * rows
    far_p = product(p_rows(2), weight_p).astype(bf16)
    far_q = product(q_rows(2), weight_q).astype(bf16)
    p_top, p_low, q_top, q_low, down_weight, head_now, down_mask_now, grid = together(
        far_p[:mid], far_p[mid:], far_q[:mid], far_q[mid:], down_weight, head_weight, down_mask, grid
    )
    p_top, p_low = shift(p_top, "x", 1), shift(p_low, "x", -1)
    q_top, q_low = shift(q_top, "z", 1), shift(q_low, "z", -1)

    p_up, p_down = join(p_rows(1), weight_p, p_top, False), join(p_rows(-1), weight_p, p_low, True)
    q_up, q_down = join(q_rows(1), weight_q, q_top, False), join(q_rows(-1), weight_q, q_low, True)
    p_up, p_down = shift(p_up, "x", 1), shift(p_down, "x", -1)
    q_up, q_down = shift(q_up, "z", 1), shift(q_down, "z", -1)

    down_kept = kept_blocks(down_weight, down_mask_now)

    def with_parts(down, token):
        high = lax.reduce_precision(token, 8, 7)
        low = (token - high).astype(bf16)
        return jnp.concatenate([down.astype(bf16), high.astype(bf16), low], axis=-2)

    small = with_parts(
        product(down_kept, head_now).reshape(16, units // 16, classes),
        product(tokens, head_now).reshape(16, own // 16, classes),
    )
    small = jnp.sum(lax.all_to_all(small, "row", 0, 0, tiled=True).astype(f32), axis=0)
    cut, last = units // 16, units // 16 + own // 16
    small, tokens_t = together(small, grid.reshape(count, width).T)
    small = to_all(with_parts(small[:cut], small[cut:last] + small[last:]), "row", 16)
    down_head = small[:, :cut].reshape(units, classes)
    token_head = (small[:, cut:last].astype(f32) + small[:, last:].astype(f32)).reshape(own, classes)

    steps = (1, -1, 2)
    sends_p, sum_p = own_pieces(p_rows(0), weight_p, p_up, p_down, z, steps)
    sends_q, sum_q = own_pieces(q_rows(0), weight_q, q_up, q_down, x, steps)
    sends = together(*sends_p, *sends_q)
    for step, send_p, send_q in zip(steps, sends[:3], sends[3:]):
        sum_p += shift(send_p, "z", step).astype(f32)
        sum_q += shift(send_q, "x", step).astype(f32)

    sum_p, sum_q, mine_p, mine_q, sides = together(
        sum_p, sum_q, sum_p.astype(bf16), sum_q.astype(bf16), jnp.transpose(down_head)
    )
    got_p = [mine_p] + [shift(mine_p, "z", step) for step in steps]
    got_q = [mine_q] + [shift(mine_q, "x", step) for step in steps]
    in_halves = lambda got: (jnp.concatenate(got[:2], axis=0), jnp.concatenate(got[2:], axis=0))
    chunk_p, chunk_q = in_halves(got_p), in_halves(got_q)
    sum_p, sum_q, *_ = together(sum_p, sum_q, got_p[1], got_q[1])

    part = jnp.zeros((rows, classes), f32)
    for sums, side in ((sum_p, down_head[:half]), (sum_q, down_head[half:])):
        gate, up = sums[:, :half], sums[:, half:]
        part += product((gate * jax.nn.sigmoid(gate) * up).astype(bf16), side)
    owner = col == row >> 1
    start = (row & 1) * rows
    part += jnp.where(owner, rows_at(token_head, start, rows), 0.0)
    label_row = jnp.where(owner, rows_at(labels, start, rows), 0).astype(f32)
    label_row = jnp.pad(label_row[None, :], ((0, 7), (0, classes - rows)))
    carried = jnp.concatenate([part, label_row], axis=0)
    carried = jnp.sum(to_all(carried, "col", 8), axis=0)

    p_top, q_top = together(chunk_p[0], chunk_q[0])
    p_low, q_low = together(chunk_p[1], chunk_q[1])
    below_p, below_q = [shift(p_top, "x", 1)], [shift(q_top, "z", 1)]
    above_p, above_q = [shift(p_top, "x", -1)], [shift(q_top, "z", -1)]
    above_p, above_q = above_p + [shift(p_low, "x", -1)], above_q + [shift(q_low, "z", -1)]
    below_p, below_q = below_p + [shift(p_low, "x", 1)], below_q + [shift(q_low, "z", 1)]
    far_p = [shift(below_p[0], "x", 1), shift(above_p[1], "x", -1)]
    far_q = [shift(below_q[0], "z", 1), shift(above_q[1], "z", -1)]
    carried = to_all(carried, "row", 16)

    dlogits_grid, costs = losses(carried, rows)
    token_loss = rows_at(costs, col * 2, 2)[:, :rows].reshape(own)
    dlogits = dlogits_grid.reshape(count, classes)
    dlogits_grid = dlogits_grid.reshape(4, 4, rows, classes)

    def spots(at, other, aways):
        return [jnp.stack([at + away, other, other - 1, other + 1, other + 2]) & 3 for away in aways]

    first_spots = jnp.concatenate(spots(x, z, (0, -1, 1)) + spots(z, x, (0, -1, 1)))
    last_spots = jnp.concatenate(spots(x, z, (2,)) + spots(z, x, (2,)))
    halves = (sides[:, :half], sides[:, half:])
    weights = (weight_p, weight_q)
    state = back_steps(
        (chunk_p, below_p, above_p), (chunk_q, below_q, above_q), first_spots, dlogits_grid, halves, weights, ()
    )
    delta_p, delta_q, inner, middle = back_steps(
        (far_p,), (far_q,), last_spots, dlogits_grid, halves, weights, state
    )

    inner = inner.reshape(4, 2, own, width)
    kept_half = pick(inner, core, 1) + shift(pick(inner, 1 - core, 1).astype(bf16), "core", 1).astype(f32)
    mine = pick(kept_half, y)
    for step in (1, -1, 2):
        mine = mine + shift(pick(kept_half, y + step).astype(bf16), "y", step).astype(f32)
    dmixed = product_t(rows_at(dlogits, col * own, own), head_weight)
    tokens_grad = (dmixed.astype(bf16).astype(f32) + mine).astype(bf16)

    by_side = lambda mask: jnp.stack(jnp.split(mask, 2, axis=1))
    masks = (by_side(gate_mask), by_side(up_mask), jnp.stack(jnp.split(down_mask, 2, axis=0)))
    grads = weight_grads(0, (), tokens_t, delta_p.reshape(count, units), middle, head_weight, *masks)
    gate_grad, up_grad, down_grad = weight_grads(
        1, grads, tokens_t, delta_q.reshape(count, units), middle, head_weight, *masks
    )
    return (token_loss, tokens_grad, gate_grad, up_grad, down_grad)


def solution(mesh):
    placed = (
        P("col", "row"),
        P("row", "col"),
        P("row", "col"),
        P("col", "row"),
        P("row", "col"),
        P("row", "col"),
        P("col", "row"),
        P("row", None),
        P("col"),
    )
    return jax.shard_map(
        shards,
        mesh=mesh,
        in_specs=placed,
        out_specs=(P("col"), P("col", "row"), P("row", "col"), P("row", "col"), P("col", "row")),
        check_vma=False,
    )
```

```python
import jax
import jax.numpy as jnp
from jax import lax
from jax.experimental import pallas as pl
from jax.experimental.pallas import tpu as pltpu
from jax.sharding import PartitionSpec as P

loss_scale = 8.0
bf16 = jnp.bfloat16
f32 = jnp.float32
block = 64


def kept_blocks(weight, block_mask):
    height, breadth = weight.shape
    lanes = jnp.repeat(block_mask.astype(weight.dtype), breadth // block_mask.shape[1], axis=1)
    tall = weight.reshape(block_mask.shape[0], height // block_mask.shape[0], breadth)
    return (tall * lanes[:, None, :]).reshape(height, breadth)


def shift(value, line, step):
    if line == "x":
        pairs = [(r, (r // 4 + step) % 4 * 4 + r % 4) for r in range(16)]
        return lax.ppermute(value, "row", pairs)
    if line == "z":
        pairs = [(r, r // 4 * 4 + (r % 4 + step) % 4) for r in range(16)]
        return lax.ppermute(value, "row", pairs)
    if line == "y":
        pairs = [(c, (c // 2 + step) % 4 * 2 + c % 2) for c in range(8)]
        return lax.ppermute(value, "col", pairs)
    return lax.ppermute(value, "col", [(c, c ^ 1) for c in range(8)])


def pick(stack, at, axis=0):
    at = at & (stack.shape[axis] - 1)
    return lax.dynamic_index_in_dim(stack, at, axis, keepdims=False, allow_negative_indices=False)


def put(stack, value, at):
    at = at & (stack.shape[0] - 1)
    return lax.dynamic_update_index_in_dim(stack, value, at, 0, allow_negative_indices=False)


def rows_at(stack, start, size):
    return lax.dynamic_slice_in_dim(stack, start, size, 0, allow_negative_indices=False)


def together(*values):
    return lax.optimization_barrier(values)


def to_all(value, axis, count):
    return lax.all_to_all(jnp.broadcast_to(value, (count,) + value.shape), axis, 0, 0, tiled=True)


def product(left, right):
    return jnp.dot(left, right, preferred_element_type=f32)


def product_t(left, right):
    return lax.dot_general(left, right, (((1,), (1,)), ((), ())), preferred_element_type=f32)


def t_product(left, right):
    return lax.dot_general(left, right, (((0,), (0,)), ((), ())), preferred_element_type=f32)


def spread_lanes(mask_ref, breadth):
    lanes = mask_ref.shape[-1]
    wide = lax.broadcasted_iota(jnp.int32, (lanes, breadth), 1)
    tall = lax.broadcasted_iota(jnp.int32, (lanes, breadth), 0) * block
    hit = jnp.where((wide >= tall) & (wide < tall + block), 1.0, 0.0)
    return product(mask_ref[...].astype(f32), hit)


def keep_kernel(gate_ref, up_ref, gate_mask, up_mask, p_ref, q_ref):
    units = gate_ref.shape[1]
    half = units // 2
    for ref, mask, left in ((gate_ref, gate_mask, 0), (up_ref, up_mask, half)):
        kept = spread_lanes(mask, units).astype(bf16)
        for k in range(mask.shape[0]):
            rows = slice(k * block, (k + 1) * block)
            value = ref[rows, :] * kept[k : k + 1, :]
            p_ref[rows, left : left + half] = value[:, :half]
            q_ref[rows, left : left + half] = value[:, half:]


def keep_weights(gate, up, gate_mask, up_mask):
    shape = jax.ShapeDtypeStruct(gate.shape, gate.dtype)
    tall = gate.shape[0]
    rows = pl.BlockSpec((tall, gate.shape[1]), lambda i: (i, 0))
    masks = pl.BlockSpec(gate_mask.shape, lambda i: (i, 0))
    return pl.pallas_call(
        keep_kernel,
        grid=(1,),
        in_specs=[rows, rows, masks, masks],
        out_specs=[rows, rows],
        out_shape=[shape, shape],
        compiler_params=pltpu.CompilerParams(vmem_limit_bytes=24 * 2**20),
        cost_estimate=pl.CostEstimate(
            flops=2 * gate.size, bytes_accessed=8 * gate.size, transcendentals=0
        ),
    )(gate, up, gate_mask, up_mask)


def join_kernel(low, rows_ref, weight_ref, got_ref, out_ref):
    half = got_ref.shape[0]
    for k in range(2):
        span = slice(k * half, (k + 1) * half)
        part = product(rows_ref[span, :], weight_ref[...])
        if low == bool(k):
            part = part + got_ref[...].astype(f32)
        out_ref[span, :] = part.astype(bf16)


def join(rows, weight, got, low):
    whole = lambda value: pl.BlockSpec(value.shape, lambda i: (0, 0))
    shape = jax.ShapeDtypeStruct((rows.shape[0], weight.shape[1]), bf16)
    return pl.pallas_call(
        lambda *refs: join_kernel(low, *refs),
        grid=(1,),
        in_specs=[whole(rows), whole(weight), whole(got)],
        out_specs=whole(shape),
        out_shape=shape,
        compiler_params=pltpu.CompilerParams(vmem_limit_bytes=16 * 2**20),
        cost_estimate=pl.CostEstimate(
            flops=2 * rows.shape[0] * weight.size, bytes_accessed=2 * weight.size, transcendentals=0
        ),
    )(rows, weight, got)


def own_kernel(at_ref, rows_ref, weight_ref, up_ref, down_ref, *refs):
    *outs, mine_ref, parts_ref = refs
    sub = mine_ref.shape[0]
    half = 2 * sub
    for k in range(2):
        span = slice(k * half, (k + 1) * half)
        part = product(rows_ref[span, :], weight_ref[...])
        part = part + up_ref[span, :].astype(f32) + down_ref[span, :].astype(f32)
        parts_ref[2 * k : 2 * k + 2] = part.reshape(2, sub, part.shape[1])
    mine_ref[...] = parts_ref[at_ref[0]]
    for k, out in enumerate(outs):
        out[...] = parts_ref[at_ref[1 + k]].astype(bf16)


def own_pieces(rows, weight, up, down, at, steps):
    sub, wide = rows.shape[0] // 4, weight.shape[1]
    spots = jnp.stack([at] + [at + step for step in steps]) & 3
    whole = lambda value: pl.BlockSpec(value.shape, lambda i, at: (0, 0))
    shapes = [jax.ShapeDtypeStruct((sub, wide), bf16)] * len(steps)
    shapes += [jax.ShapeDtypeStruct((sub, wide), f32)]
    *sends, mine = pl.pallas_call(
        own_kernel,
        grid_spec=pltpu.PrefetchScalarGridSpec(
            num_scalar_prefetch=1,
            grid=(1,),
            in_specs=[whole(value) for value in (rows, weight, up, down)],
            out_specs=[whole(shape) for shape in shapes],
            scratch_shapes=[pltpu.VMEM((4, sub, wide), f32)],
        ),
        out_shape=shapes,
        compiler_params=pltpu.CompilerParams(vmem_limit_bytes=20 * 2**20),
        cost_estimate=pl.CostEstimate(
            flops=2 * rows.shape[0] * weight.size, bytes_accessed=4 * weight.size, transcendentals=0
        ),
    )(spots, rows, weight, up, down)
    return sends, mine


def loss_kernel(carried_ref, dlogits_ref, cost_ref):
    rows, classes = dlogits_ref.shape[1:]
    tall = lax.broadcasted_iota(jnp.int32, (rows, classes), 0)
    wide = lax.broadcasted_iota(jnp.int32, (rows, classes), 1)
    for k in range(dlogits_ref.shape[0]):
        logits = carried_ref[k, :rows, :]
        label_row = carried_ref[k, rows : rows + 1, :]
        label = jnp.sum(jnp.where(tall == wide, label_row, 0.0), axis=1, keepdims=True)
        onehot = jnp.where(label.astype(jnp.int32) == wide, 1.0, 0.0)
        exponent = jnp.exp(logits)
        partition = jnp.sum(exponent, axis=1, keepdims=True)
        cost = jnp.log(partition) - jnp.sum(logits * onehot, axis=1, keepdims=True)
        cost_ref[k : k + 1, :] = jnp.sum(jnp.where(tall == wide, cost, 0.0), axis=0, keepdims=True)
        dlogits_ref[k] = (loss_scale * (exponent / partition - onehot)).astype(bf16)


def losses(carried, rows):
    groups, _, classes = carried.shape
    whole = lambda shape: pl.BlockSpec(shape, lambda i: (0,) * len(shape))
    return pl.pallas_call(
        loss_kernel,
        grid=(1,),
        in_specs=[whole(carried.shape)],
        out_specs=[whole((groups, rows, classes)), whole((groups, classes))],
        out_shape=[
            jax.ShapeDtypeStruct((groups, rows, classes), bf16),
            jax.ShapeDtypeStruct((groups, classes), f32),
        ],
        compiler_params=pltpu.CompilerParams(vmem_limit_bytes=8 * 2**20),
        cost_estimate=pl.CostEstimate(
            flops=20 * carried.size, bytes_accessed=8 * carried.size, transcendentals=carried.size
        ),
    )(carried)


def back_kernel(stacked, count, again, at_ref, *refs):
    stack_ref, refs = (refs[0], refs[1:]) if stacked else (None, refs)
    sums, refs = refs[: 2 * count], refs[2 * count :]
    dlogits_ref, refs = refs[0], refs[1:]
    if stacked:
        sides, weights, refs = refs[:2], refs[2:4], refs[4:]
    else:
        sides, weights, refs = (None, refs[0]), (None, refs[1]), refs[2:]
    before = refs[1:3] if again else ()
    inner_ref, middle_ref, dlogits_flat, hidden_flat, delta_flat = refs[-5:]
    deltas = refs[-7:-5] if stacked else (None, refs[-6])
    units = sides[1].shape[0]
    rows = delta_flat.shape[0]
    sub = rows // 4
    now = pl.program_id(0)

    @pl.when(now == 0)
    def _():
        inner_ref[...] = before[0][...] if again else jnp.zeros(inner_ref.shape, f32)
        middle_ref[...] = before[1][...] if again else jnp.zeros(middle_ref.shape, f32)

    def chunk(part, step, pair):
        chunk_at = at_ref[5 * step]
        others = [at_ref[5 * step + 1 + k] for k in range(4)]
        places = [(chunk_at, other) if part == 0 else (other, chunk_at) for other in others]
        local = [(0, other) if part == 0 else (other, 0) for other in others]
        for k in range(4):
            dlogits_flat[k * sub : (k + 1) * sub, :] = dlogits_ref[places[k]]
        tall = rows // 2
        for top, source in ((0, pair[0]), (tall, pair[1])):
            for left in range(0, units, 128):
                gate = source[:, left : left + 128].astype(f32)
                up = source[:, units + left : units + left + 128].astype(f32)
                dhidden = product_t(dlogits_flat[top : top + tall, :], sides[part][left : left + 128, :])
                sigmoid_gate = 0.5 * jnp.tanh(0.5 * gate) + 0.5
                activated = gate * sigmoid_gate
                hidden_flat[top : top + tall, left : left + 128] = (activated * up).astype(bf16)
                gate_delta = dhidden * up * sigmoid_gate * (1.0 + gate * (1.0 - sigmoid_gate))
                delta_flat[top : top + tall, left : left + 128] = gate_delta.astype(bf16)
                delta_flat[top : top + tall, units + left : units + left + 128] = (
                    dhidden * activated
                ).astype(bf16)
        inner = product_t(delta_flat[...], weights[part][...])
        for k in range(4):
            span = slice(k * sub, (k + 1) * sub)
            deltas[part][local[k]] = delta_flat[span, :]
            inner_ref[places[k]] = inner_ref[places[k]] + inner[span]
        middle_ref[part] = middle_ref[part] + t_product(dlogits_flat[...], hidden_flat[...])

    if stacked:
        pl.when(now < stacked)(lambda: chunk(0, now, (stack_ref.at[0], stack_ref.at[1])))
    for k in range(count):
        step = stacked + k
        pl.when(now == step)(lambda k=k, step=step: chunk(1, step, sums[2 * k : 2 * k + 2]))


def back_steps(stack, chunks, spots, dlogits, sides, weights, before):
    pieces = [half for pair in chunks for half in pair]
    count = len(chunks)
    tall, wide = pieces[0].shape
    stacked = 0 if stack is None else stack.shape[0] // 2
    rows = 2 * tall
    sub = rows // 4
    classes = dlogits.shape[-1]
    width, units = weights[0].shape[0], sides.shape[0] // 2

    def whole(value, **mode):
        return pl.BlockSpec(value.shape, lambda i, at: (0,) * len(value.shape), **mode)

    once = dict(pipeline_mode=pl.Buffered(1))
    side = lambda part: pl.BlockSpec((units, classes), lambda i, at: (part, 0), **once)
    which = (0, 1) if stacked else (1,)
    fixed = [*pieces, dlogits, *[sides for _ in which], *weights]
    in_specs = [whole(value, **once) for value in (*pieces, dlogits)]
    in_specs += [side(part) for part in which] + [whole(value, **once) for value in weights]
    shapes = [
        pltpu.HBM((4, 4, sub, wide), bf16),
        pltpu.HBM((4, 4, sub, width), f32),
        pltpu.HBM((2, classes, units), f32),
    ]
    out_specs = [
        pl.BlockSpec((4, 1, sub, wide), lambda i, at: (0, at[5 * jnp.maximum(i, stacked)], 0, 0)),
        whole(shapes[1]),
        whole(shapes[2]),
    ]
    if stacked:
        fixed = [stack] + fixed
        in_specs = [
            pl.BlockSpec((2, tall, wide), lambda i, at: (jnp.minimum(i, stacked - 1), 0, 0))
        ] + in_specs
        shapes = [shapes[0]] + shapes
        out_specs = [
            pl.BlockSpec(
                (1, 4, sub, wide), lambda i, at: (at[5 * jnp.minimum(i, stacked - 1)], 0, 0, 0)
            )
        ] + out_specs
    aliases = {}
    if before:
        in_specs += [pl.BlockSpec(memory_space=pl.ANY)] + [whole(value, **once) for value in before[1:]]
        aliases = {1 + len(fixed) + k: len(shapes) - 3 + k for k in range(3)}
    steps = stacked + count
    return pl.pallas_call(
        lambda *refs: back_kernel(stacked, count, bool(before), *refs),
        grid_spec=pltpu.PrefetchScalarGridSpec(
            num_scalar_prefetch=1,
            grid=(steps,),
            in_specs=in_specs,
            out_specs=out_specs,
            scratch_shapes=[
                pltpu.VMEM((rows, classes), bf16),
                pltpu.VMEM((rows, units), bf16),
                pltpu.VMEM((rows, wide), bf16),
            ],
        ),
        out_shape=shapes,
        input_output_aliases=aliases,
        compiler_params=pltpu.CompilerParams(vmem_limit_bytes=60 * 2**20),
        cost_estimate=pl.CostEstimate(
            flops=2 * steps * rows * (wide * width + 2 * units * classes),
            bytes_accessed=steps * 4 * rows * wide + 4 * wide * width,
            transcendentals=steps * rows * units,
        ),
    )(spots, *fixed, *before)


def grad_kernel(tokens_ref, delta_ref, middle_ref, head_ref, gate_mask, up_mask, down_mask, *refs):
    gate_ref, up_ref, down_ref = refs[-3:]
    units = gate_ref.shape[1]
    for ref, mask, left in ((gate_ref, gate_mask, 0), (up_ref, up_mask, units)):
        grad = product(tokens_ref[...], delta_ref[:, left : left + units])
        lanes = spread_lanes(mask.at[0], units)
        grad = grad.reshape(lanes.shape[0], block, units) * lanes[:, None, :]
        ref[...] = grad.reshape(ref.shape).astype(bf16)
    down = lax.dot_general(
        middle_ref[0].astype(bf16), head_ref[...], (((0,), (1,)), ((), ())), preferred_element_type=f32
    )
    lanes = spread_lanes(down_mask.at[0], down.shape[1])
    down = down.reshape(lanes.shape[0], block, down.shape[1]) * lanes[:, None, :]
    down_ref[...] = down.reshape(down_ref.shape).astype(bf16)


def weight_grads(part, before, tokens_t, delta, middle, head, gate_mask, up_mask, down_mask):
    width, count = tokens_t.shape
    units = middle.shape[2]
    wide = 2 * units
    fixed = lambda value: pl.BlockSpec(value.shape, lambda i: (0,) * len(value.shape))
    lead = lambda value: pl.BlockSpec((1,) + value.shape[1:], lambda i: (part, 0, 0))
    side = pl.BlockSpec((width, units), lambda i: (0, part))
    return pl.pallas_call(
        grad_kernel,
        grid=(1,),
        in_specs=[
            fixed(tokens_t),
            fixed(delta),
            lead(middle),
            fixed(head),
            lead(gate_mask),
            lead(up_mask),
            lead(down_mask),
        ]
        + [pl.BlockSpec(memory_space=pl.ANY)] * len(before),
        out_specs=[side, side, pl.BlockSpec((units, width), lambda i: (part, 0))],
        out_shape=[
            jax.ShapeDtypeStruct((width, wide), bf16),
            jax.ShapeDtypeStruct((width, wide), bf16),
            jax.ShapeDtypeStruct((wide, width), bf16),
        ],
        input_output_aliases={7 + k: k for k in range(len(before))},
        compiler_params=pltpu.CompilerParams(vmem_limit_bytes=60 * 2**20),
        cost_estimate=pl.CostEstimate(
            flops=2 * count * wide * width, bytes_accessed=4 * count * wide, transcendentals=0
        ),
    )(tokens_t, delta, middle, head, gate_mask, up_mask, down_mask, *before)


def shards(
    tokens, gate_weight, up_weight, down_weight, gate_mask, up_mask, down_mask, head_weight, labels
):
    row, col = lax.axis_index("row"), lax.axis_index("col")
    x, z, y, core = row >> 2, row & 3, col >> 1, col & 1
    own, width = tokens.shape
    units = gate_weight.shape[1]
    half = units // 2
    count = own * 8
    rows = count // 16
    classes = head_weight.shape[1]

    mates = put(jnp.zeros((4, own, width), bf16), tokens, y)
    for step in (1, -1, 2):
        mates = put(mates, shift(tokens, "y", step), y - step)
    others = shift(mates, "core", 1)
    first = core == 0
    every = jnp.stack([jnp.where(first, mates, others), jnp.where(first, others, mates)], axis=1)
    every = every.reshape(count, width)
    grid = every.reshape(4, 4, rows, width)

    weight_p, weight_q = keep_weights(gate_weight, up_weight, gate_mask, up_mask)

    lines = [[z + 4 * x for x in range(4)] for z in range(4)]
    part_p = product(every, weight_p).astype(bf16)
    sum_p = lax.psum_scatter(part_p, "row", scatter_dimension=0, axis_index_groups=lines, tiled=True)
    q_rows = lambda away: pick(grid, z + away, 1).reshape(4 * rows, width)
    mid = 2 * rows
    far_q = product(q_rows(2), weight_q).astype(bf16)
    q_top, q_low, down_weight, head_now, down_mask_now, grid = together(
        far_q[:mid], far_q[mid:], down_weight, head_weight, down_mask, grid
    )
    q_top, q_low = shift(q_top, "z", 1), shift(q_low, "z", -1)
    q_up, q_down = join(q_rows(1), weight_q, q_top, False), join(q_rows(-1), weight_q, q_low, True)
    q_up, q_down = shift(q_up, "z", 1), shift(q_down, "z", -1)

    down_kept = kept_blocks(down_weight, down_mask_now)

    def with_parts(down, token):
        high = lax.reduce_precision(token, 8, 7)
        low = (token - high).astype(bf16)
        return jnp.concatenate([down.astype(bf16), high.astype(bf16), low], axis=-2)

    small = with_parts(
        product(down_kept, head_now).reshape(16, units // 16, classes),
        product(tokens, head_now).reshape(16, own // 16, classes),
    )
    small = jnp.sum(lax.all_to_all(small, "row", 0, 0, tiled=True).astype(f32), axis=0)
    cut, last = units // 16, units // 16 + own // 16
    small, tokens_t = together(small, grid.reshape(count, width).T)
    small = to_all(with_parts(small[:cut], small[cut:last] + small[last:]), "row", 16)
    down_head = small[:, :cut].reshape(units, classes)
    token_head = (small[:, cut:last].astype(f32) + small[:, last:].astype(f32)).reshape(own, classes)

    steps = (1, -1, 2)
    sum_p, q_up, q_down = together(sum_p, q_up, q_down)
    sum_p = sum_p.reshape(4, rows, units)
    sends_p = [pick(sum_p, z + step) for step in steps]
    sum_p = pick(sum_p, z).astype(f32)
    sends_q, sum_q = own_pieces(q_rows(0), weight_q, q_up, q_down, x, steps)
    sends = together(*sends_p, *sends_q)
    for step, send_p, send_q in zip(steps, sends[:3], sends[3:]):
        sum_p += shift(send_p, "z", step).astype(f32)
        sum_q += shift(send_q, "x", step).astype(f32)

    sum_p, sum_q, mine_p, mine_q, down_head, token_head = together(
        sum_p, sum_q, sum_p.astype(bf16), sum_q.astype(bf16), down_head, token_head
    )
    got_p = [mine_p] + [shift(mine_p, "z", step) for step in steps]
    got_q = [mine_q] + [shift(mine_q, "x", step) for step in steps]
    chunk_p = jnp.concatenate(got_p, axis=0)
    chunk_q = jnp.concatenate(got_q[:2], axis=0), jnp.concatenate(got_q[2:], axis=0)
    sum_p, sum_q, chunk_p = together(sum_p, sum_q, chunk_p)
    stack_p = lax.all_gather(chunk_p, "row", axis=0, axis_index_groups=lines, tiled=True)

    part = jnp.zeros((rows, classes), f32)
    for sums, side in ((sum_p, down_head[:half]), (sum_q, down_head[half:])):
        gate, up = sums[:, :half], sums[:, half:]
        part += product((gate * jax.nn.sigmoid(gate) * up).astype(bf16), side)
    owner = col == row >> 1
    start = (row & 1) * rows
    part += jnp.where(owner, rows_at(token_head, start, rows), 0.0)
    label_row = jnp.where(owner, rows_at(labels, start, rows), 0).astype(f32)
    label_row = jnp.pad(label_row[None, :], ((0, 7), (0, classes - rows)))
    carried = jnp.concatenate([part, label_row], axis=0)
    carried = jnp.sum(to_all(carried, "col", 8), axis=0)

    q_top, q_low = chunk_q
    below_q = [shift(q_top, "z", 1), shift(q_low, "z", 1)]
    above_q = [shift(q_top, "z", -1), shift(q_low, "z", -1)]
    far_q = [shift(below_q[0], "z", 1), shift(above_q[1], "z", -1)]
    carried = to_all(carried, "row", 16)

    dlogits_grid, costs = losses(carried, rows)
    token_loss = rows_at(costs, col * 2, 2)[:, :rows].reshape(own)
    dlogits = dlogits_grid.reshape(count, classes)
    dlogits_grid = dlogits_grid.reshape(4, 4, rows, classes)

    def spots(at, other, aways):
        return [jnp.stack([at + away, other, other - 1, other + 1, other + 2]) & 3 for away in aways]

    first_spots = jnp.concatenate(spots(z, x, (0, -1, 1)))
    last_spots = jnp.concatenate(spots(0, z, range(4)) + spots(z, x, (2,)))
    state = back_steps(
        None, (chunk_q, below_q, above_q), first_spots, dlogits_grid, down_head, (weight_q,), ()
    )
    dmixed = product_t(rows_at(dlogits, col * own, own), head_weight).astype(bf16)
    stack_p, dmixed, token_loss = together(stack_p.reshape(8, mid, units), dmixed, token_loss)
    delta_p, delta_q, inner, middle = back_steps(
        stack_p, (far_q,), last_spots, dlogits_grid, down_head, (weight_p, weight_q), state
    )

    inner = inner.reshape(4, 2, own, width)
    kept_half = pick(inner, core, 1) + shift(pick(inner, 1 - core, 1).astype(bf16), "core", 1).astype(f32)
    mine = pick(kept_half, y)
    for step in (1, -1, 2):
        mine = mine + shift(pick(kept_half, y + step).astype(bf16), "y", step).astype(f32)
    tokens_grad = (dmixed.astype(f32) + mine).astype(bf16)

    by_side = lambda mask: jnp.stack(jnp.split(mask, 2, axis=1))
    masks = (by_side(gate_mask), by_side(up_mask), jnp.stack(jnp.split(down_mask, 2, axis=0)))
    grads = weight_grads(0, (), tokens_t, delta_p.reshape(count, units), middle, head_weight, *masks)
    gate_grad, up_grad, down_grad = weight_grads(
        1, grads, tokens_t, delta_q.reshape(count, units), middle, head_weight, *masks
    )
    return (token_loss, tokens_grad, gate_grad, up_grad, down_grad)


def solution(mesh):
    placed = (
        P("col", "row"),
        P("row", "col"),
        P("row", "col"),
        P("col", "row"),
        P("row", "col"),
        P("row", "col"),
        P("col", "row"),
        P("row", None),
        P("col"),
    )
    return jax.shard_map(
        shards,
        mesh=mesh,
        in_specs=placed,
        out_specs=(P("col"), P("col", "row"), P("row", "col"), P("row", "col"), P("col", "row")),
        check_vma=False,
    )
```
